32 devices in a mesh: row: 8 (over z, x), col: 4 (over y, core).
Axes of the slice: x: 2, y: 2, z: 4, core: 2. Of those that a mesh axis runs over, the one named last changes fastest.
Arguments:
- amplitudes: bfloat16 [1024, 8192], P('row', 'col'), may hold values from -6 to 6
- integrals: bfloat16 [8192, 16384], P('col', 'row'), may hold values from -0.125 to 0.125
- tile_irrep: int32 [24], replicated, may hold values from 0 to 3
- product_pairs: int32 [64, 2], P('row'), may hold values from 0 to 23, as said below
- summed_pairs: int32 [32, 2], P('col'), may hold values from 0 to 23, as said below
Outputs:
- residual: bfloat16 [1024, 16384], P('col', 'row')
The draws below stay inside these ranges and needn't reach their ends.
Inputs may be any that keep to these rules, and one draw needn't show every extreme that they name: `product_pairs`: for p < 32, entry p + 32 holds the two tiles of entry p in swapped order; the two tiles of an entry differ; no entry repeats. `summed_pairs`: no entry repeats.
All inputs are finite; a program needn't handle non-finite values.
Results may differ from the reference program's by a relative error of at most 0.001.
Values may be sent and summed in bfloat16 or wider, within the bound.
No kernel may reach another device: no remote copies, remote signals or barrier semaphores. Data moves between devices by JAX's collectives and lax.ppermute only.
A program may use at most 192 MiB of HBM per device.

```python
import jax
import jax.numpy as jnp
import numpy as np
from jax import lax

TS = 16
TP = 256
NT = 24
OT = 32
OP = 1024
NPC = 32
NPA = 64


def draw_product_pairs(key, part):
    upper_first, upper_second = np.triu_indices(NT, 1)
    first = jnp.asarray(upper_first, dtype=jnp.int32)
    second = jnp.asarray(upper_second, dtype=jnp.int32)
    order = jax.random.permutation(key, first.shape[0])[:NPA // 2]
    left = first[order]
    right = second[order]
    flipped = jax.random.randint(jax.random.fold_in(key, 7), (NPA // 2,), 0, 2)
    head_first = jnp.where(flipped == 1, right, left)
    head_second = jnp.where(flipped == 1, left, right)
    head = jnp.stack([head_first, head_second], axis=1)
    tail = jnp.stack([head_second, head_first], axis=1)
    return jnp.concatenate([head, tail], axis=0).astype(jnp.int32)


def draw_summed_pairs(key, part):
    order = jax.random.permutation(key, NT * NT)[:NPC].astype(jnp.int32)
    return jnp.stack([order // NT, order % NT], axis=1).astype(jnp.int32)


def place_ends(result, key, low, top_value):
    extent = result.shape
    spot = [jax.random.randint(jax.random.fold_in(key, axis), (), 0, extent[axis]) for axis in range(len(extent))]
    result = result.at[tuple(spot)].set(low)
    longest = extent.index(max(extent))
    spot[longest] = (spot[longest] + 1) % extent[longest]
    return result.at[tuple(spot)].set(top_value)


def block_scale(key, extent, pieces, smallest, high):
    level, own = 1.0, jax.random.fold_in(key, 6)
    for position, parts in pieces:
        heights = jnp.exp(jax.random.uniform(jax.random.fold_in(own, position), (parts,), jnp.float32, smallest / len(pieces), high / len(pieces)))
        level = level * jnp.repeat(heights, extent[position] // parts).reshape([-1 if axis == position else 1 for axis in range(len(extent))])
    return level


def noise(own_key, dims, width, reach, cuts=(), kind=jnp.bfloat16):
    result = jax.random.normal(own_key, dims, jnp.float32) * width
    if len(cuts) > 0:
        result = block_scale(own_key, dims, cuts, -0.22, 0.18) * result
    return jnp.clip(result, min=-reach, max=reach).astype(kind)


def setup_inputs(seed: int = 0) -> dict:
    seeds = jax.random.split(jax.random.key(seed), 6)
    return {
        "amplitudes": noise(seeds[0], (OP, NPC * TP), 1.0, 6.0, ((0, 8), (1, 4))),
        "integrals": noise(seeds[1], (NPC * TP, NPA * TP), (NPC * TP // 4) ** -0.5, 0.125, ((0, 4), (1, 8))),
        "tile_irrep": place_ends(jax.random.randint(seeds[2], (NT,), 0, 4), jax.random.fold_in(seeds[2], 1), 0, 3).astype(jnp.int32),
        "product_pairs": draw_product_pairs(jax.random.fold_in(seeds[5], 71), 0),
        "summed_pairs": draw_summed_pairs(jax.random.fold_in(seeds[5], 71), 0),
    }


def pair_symmetry(tile_irrep, pairs):
    return jnp.bitwise_xor(tile_irrep[pairs[:, 0]], tile_irrep[pairs[:, 1]])


def reference(amplitudes, integrals, tile_irrep, product_pairs, summed_pairs):
    product_sym = pair_symmetry(tile_irrep, product_pairs)
    summed_sym = pair_symmetry(tile_irrep, summed_pairs)
    allowed = summed_sym[:, None] == product_sym[None, :]

    def one_block(index):
        keep = jnp.repeat(allowed[:, index], TP).astype(amplitudes.dtype)
        masked = amplitudes * keep[None, :]
        panel = lax.dynamic_slice_in_dim(integrals, index * TP, TP, 1)
        return jnp.dot(masked, panel, preferred_element_type=jnp.float32)

    blocks = lax.map(one_block, jnp.arange(NPA, dtype=jnp.int32))
    ladder = jnp.transpose(blocks, (1, 0, 2)).reshape(OT, OT, NPA, TS, TS)
    partner = jnp.roll(ladder, NPA // 2, axis=2)
    partner = jnp.transpose(partner, (1, 0, 2, 4, 3))
    return (ladder + partner).reshape(OT * OT, NPA * TP).astype(jnp.bfloat16)
```

```python
import functools

import jax
import jax.numpy as jnp
import numpy as np
from jax import lax
from jax.experimental import pallas as pl
from jax.experimental.pallas import tpu as pltpu
from jax.sharding import PartitionSpec as P

TS = 16
TP = TS * TS
OT = 32
WIRE = jnp.float16
LADDER_VMEM = 16 * 2**20


def from_partner(value, axis, distance):
    mask = 2**distance
    pairs = [(source, source ^ mask) for source in range(lax.axis_size(axis))]
    return lax.ppermute(value, axis, pairs)


def pair_symmetry(tile_irrep, pairs):
    return jnp.bitwise_xor(tile_irrep[pairs[:, 0]], tile_irrep[pairs[:, 1]])


def plain(amplitudes, integrals, tile_irrep, product_pairs, summed_pairs):
    product_sym = pair_symmetry(tile_irrep, product_pairs)
    summed_sym = pair_symmetry(tile_irrep, summed_pairs)
    allowed = summed_sym[:, None] == product_sym[None, :]
    summed_count = summed_pairs.shape[0]
    product_count = product_pairs.shape[0]
    keep = allowed.astype(integrals.dtype)
    masked = (
        integrals.reshape(summed_count, TP, product_count, TP)
        * keep[:, None, :, None]
    ).reshape(integrals.shape)
    half_bit = lax.axis_size("row").bit_length() - 2
    ladder = jnp.dot(
        lax.all_gather(amplitudes, "row", axis=0, tiled=True),
        masked,
        preferred_element_type=jnp.float32,
    )
    partner = from_partner(ladder, "row", half_bit)
    partner = partner.reshape(OT, OT, product_count, TS, TS)
    partner = jnp.transpose(partner, (1, 0, 2, 4, 3)).reshape(ladder.shape)
    summed = lax.psum_scatter(ladder + partner, "col", scatter_dimension=0, tiled=True)
    return summed.astype(jnp.bfloat16)


NZ, NX, NY, NC = 4, 2, 2, 2
ROWS = 128
PART = 64
OWNED = 256
PLANES = ((0, 1, 2, 3), (1, 0, 2, 3), (2, 3, 1, 0), (3, 2, 1, 0))


def selection(source_of_row):
    n = len(source_of_row)
    matrix = np.zeros((n, n), np.float32)
    matrix[np.arange(n), source_of_row] = 1
    return matrix


def order_of(extents, axes):
    return np.arange(int(np.prod(extents))).reshape(extents).transpose(axes).reshape(-1)


BLOCK = selection(order_of((4, 32), (1, 0)))
ALIGN = selection(order_of((2, 2, 4, 4), (1, 0, 3, 2)))
NATURAL = selection(order_of((4, 2, 8, 4), (1, 3, 0, 2)))
SWAP = selection(order_of((16, 16), (1, 0)))


def send(value, target):
    pairs = []
    for n, (z, x, y, k) in enumerate(np.ndindex(NZ, NX, NY, NC)):
        to = target(z, x, y, k)
        if to is not None:
            pairs.append((n, int(np.ravel_multi_index(to, (NZ, NX, NY, NC)))))
    return lax.ppermute(value, ("row", "col"), pairs)


def along_z(value, moves):
    return send(value, lambda z, x, y, k: (moves[z], x, y, k) if z in moves else None)


def across_x(value):
    return send(value, lambda z, x, y, k: (z, 1 - x, y, k))


def across_y(value):
    return send(value, lambda z, x, y, k: (z, x, 1 - y, k))


def across_core(value):
    return send(value, lambda z, x, y, k: (z, x, y, 1 - k))


def to_partner(value):
    return send(value, lambda z, x, y, k: (z ^ 2, x, y, k))


def to_owner(value, step):
    def target(z, x, y, k):
        plane = PLANES[z][step]
        return (z, x, 1 - y, k) if (1 - y, k) == (plane // NC, plane % NC) else None

    return send(value, target)


def matmul(a, b):
    return jnp.dot(a, b, preferred_element_type=jnp.float32)


def part_at(distance):
    return distance ^ (distance >> 1)


def ladder_kernel(place, irrep, product, summed, here, beside, block_order, integrals, *refs):
    out, rows = refs[-2:]
    x, col = place[0] % NX, place[1]
    for block, at in ((here, x), (beside, 1 - x)):
        start = pl.multiple_of(at * ROWS, ROWS)
        rows[pl.ds(start, ROWS), :] = matmul(block_order[...], block[...]).astype(jnp.bfloat16)
    for panel in range(8):
        wanted = irrep[product[panel, 0]] ^ irrep[product[panel, 1]]
        kept = []
        for q in range(8):
            same = (irrep[summed[q, 0]] ^ irrep[summed[q, 1]]) == wanted
            value = rows[:, q * TP : (q + 1) * TP]
            kept.append(jnp.where(same, value, jnp.zeros_like(value)))
        cut = slice(panel * TP, (panel + 1) * TP)
        total = matmul(jnp.concatenate(kept, axis=1), integrals[:, cut])
        for to in range(4):
            for at in range(2):
                start = at * ROWS + to * 32
                out[part_at(to ^ col), at * 32 : (at + 1) * 32, cut] = total[start : start + 32, :]


def partial_ladder(place, irrep, product, summed, here, beside, integrals, after):
    vmem = pl.BlockSpec(memory_space=pltpu.VMEM)
    smem = pl.BlockSpec(memory_space=pltpu.SMEM)
    return pl.pallas_call(
        ladder_kernel,
        in_specs=[smem] * 4 + [vmem] * 4 + [pl.BlockSpec(memory_space=pl.ANY)] * len(after),
        out_specs=vmem,
        scratch_shapes=[pltpu.VMEM((2 * ROWS, 2048), jnp.bfloat16)],
        out_shape=jax.ShapeDtypeStruct((4, PART, 2048), jnp.float32),
        compiler_params=pltpu.CompilerParams(vmem_limit_bytes=LADDER_VMEM),
        cost_estimate=pl.CostEstimate(flops=1000, bytes_accessed=1000, transcendentals=0),
        name="partial_ladder",
    )(place, irrep, product, summed, here, beside, jnp.asarray(BLOCK, jnp.bfloat16), integrals, *after)


def turn(arrived, align, swap):
    high = arrived.astype(jnp.bfloat16)
    low = (arrived - high.astype(jnp.float32)).astype(jnp.bfloat16)
    both = jnp.concatenate([high, low], axis=0)
    cuts = [both[:, p * TP : (p + 1) * TP] for p in range(8)]
    both = jnp.concatenate([matmul(cut, swap).astype(jnp.bfloat16) for cut in cuts], axis=1)
    return matmul(align, both[:PART]) + matmul(align, both[PART:])


def turn_kernel(arrived, align, swap, out):
    out[...] = turn(arrived[...], align[...], swap[...])


def turned(arrived):
    return pl.pallas_call(
        turn_kernel,
        out_shape=jax.ShapeDtypeStruct((PART, 2048), jnp.float32),
        compiler_params=pltpu.CompilerParams(vmem_limit_bytes=12 * 2**20),
        name="turn",
    )(arrived, *(jnp.asarray(m, jnp.bfloat16) for m in (ALIGN, SWAP)))


def finish_kernel(place, *refs):
    pairs, mines, (rest, turned0, turned1, turned2, last, align, natural, swap, out, own, other, total, sems) = refs[:4], refs[4:8], refs[8:]
    z, col = place[0] // NX, place[1]

    def plane_of(side, step):
        plane = PLANES[0][step]
        for at in (1, 2, 3):
            plane = jnp.where(side == at, PLANES[at][step], plane)
        return plane

    def copies(step):
        return (
            pltpu.make_async_copy(pairs[step].at[1:4], own.at[1:4], sems.at[0]),
            pltpu.make_async_copy(mines[step], own.at[0], sems.at[1]),
        )

    for step in range(4):

        @pl.when(plane_of(z, step) == col)
        def _(step=step):
            for copy in copies(step):
                copy.start()

    for step, ref in enumerate((turned0, turned1, turned2, None)):
        value = turn(last[...], align[...], swap[...]) if ref is None else ref[...]
        other[plane_of(z ^ 2, step)] = value
    for copy in copies(0):
        copy.wait()
    for n in range(4):
        plane = part_at(n) ^ col
        value = own[n] + other[plane]
        if n > 0:
            value += rest[3 - n]
        total[pl.ds(pl.multiple_of(plane * PART, PART), PART), :] = value.astype(jnp.bfloat16)
    for p in range(8):
        cut = slice(p * TP, (p + 1) * TP)
        out[:, cut] = matmul(natural[...], total[:, cut]).astype(jnp.bfloat16)


def finish(place, pairs, mines, rest, done, last):
    vmem = pl.BlockSpec(memory_space=pltpu.VMEM)
    return pl.pallas_call(
        finish_kernel,
        in_specs=[pl.BlockSpec(memory_space=pltpu.SMEM)] + [pl.BlockSpec(memory_space=pl.ANY)] * 8 + [vmem] * 8,
        out_specs=vmem,
        out_shape=jax.ShapeDtypeStruct((OWNED, 2048), jnp.bfloat16),
        scratch_shapes=[
            pltpu.VMEM((4, PART, 2048), jnp.float32),
            pltpu.VMEM((4, PART, 2048), jnp.float32),
            pltpu.VMEM((OWNED, 2048), jnp.bfloat16),
            pltpu.SemaphoreType.DMA((2,)),
        ],
        compiler_params=pltpu.CompilerParams(vmem_limit_bytes=24 * 2**20),
        name="finish",
    )(place, *pairs, *mines, rest, *done, last, *(jnp.asarray(m, jnp.bfloat16) for m in (ALIGN, NATURAL, SWAP)))


def encode(value):
    return value.astype(WIRE)


def decode(value):
    return value.astype(jnp.float32)


def after(value, *tokens):
    return lax.optimization_barrier((value, *tokens))[0]


def on_device(amplitudes, integrals, tile_irrep, product_pairs, summed_pairs):
    row, col = lax.axis_index("row"), lax.axis_index("col")
    z = row // NX
    place = jnp.stack([row, col]).astype(jnp.int32)
    inner = (z == 1) | (z == 2)

    here, beside = [amplitudes], [across_x(amplitudes)]
    near = along_z(amplitudes, {0: 1, 1: 0, 2: 3, 3: 2})
    middle = along_z(amplitudes, {1: 2, 2: 1})
    here.append(near)
    beside.append(across_x(near))
    crossed = along_z(near, {1: 2, 2: 1})
    here.append(jnp.where(inner, middle, along_z(middle, {1: 0, 2: 3})))
    beside.append(across_x(here[2]))
    here.append(jnp.where(inner, crossed, along_z(crossed, {1: 0, 2: 3})))
    beside.append(across_x(here[3]))
    arrived = ((near, middle), (here[2], crossed), (here[3],), ())

    pairs, mines, others = [], [], []
    rest = 0
    tokens = ()
    for step in range(4):
        part = partial_ladder(place, tile_irrep, product_pairs, summed_pairs, here[step], beside[step], integrals, arrived[step] + tokens)
        sibling = across_core(part)
        if step > 0:
            mines.append(pairs[-1][0] + decode(over_y))
            sent = encode(mines[-1])
            others.append(to_partner(sent))
            part = after(part, sent)
        part = (part.reshape(2, 2, PART, 2048) + sibling.reshape(2, 2, PART, 2048)[:, ::-1]).reshape(part.shape)
        pairs.append(part)
        sent = encode(part[3])
        tokens = (part,)
        over_y = across_y(sent)
        rest = rest + to_owner(encode(part[:3]), step)
    mines.append(pairs[-1][0] + decode(over_y))
    others.append(to_partner(encode(mines[-1])))
    done = [turned(decode(other)) for other in others[:3]]
    return finish(place, pairs, mines, decode(rest), done, decode(others[3]))


def solution(mesh):
    body = on_device if (mesh.shape["row"], mesh.shape["col"]) == (NZ * NX, NY * NC) else plain
    return jax.shard_map(
        body,
        mesh=mesh,
        in_specs=(P("row", "col"), P("col", "row"), P(), P("row", None), P("col", None)),
        out_specs=P("col", "row"),
        check_vma=False,
    )
```

```python
import functools

import jax
import jax.numpy as jnp
import numpy as np
from jax import lax
from jax.experimental import pallas as pl
from jax.experimental.pallas import tpu as pltpu
from jax.sharding import PartitionSpec as P

TS = 16
TP = TS * TS
OT = 32
WIRE = jnp.float16


def from_partner(value, axis, distance):
    mask = 2**distance
    pairs = [(source, source ^ mask) for source in range(lax.axis_size(axis))]
    return lax.ppermute(value, axis, pairs)


def pair_symmetry(tile_irrep, pairs):
    return jnp.bitwise_xor(tile_irrep[pairs[:, 0]], tile_irrep[pairs[:, 1]])


def plain(amplitudes, integrals, tile_irrep, product_pairs, summed_pairs):
    product_sym = pair_symmetry(tile_irrep, product_pairs)
    summed_sym = pair_symmetry(tile_irrep, summed_pairs)
    allowed = summed_sym[:, None] == product_sym[None, :]
    summed_count = summed_pairs.shape[0]
    product_count = product_pairs.shape[0]
    keep = allowed.astype(integrals.dtype)
    masked = (
        integrals.reshape(summed_count, TP, product_count, TP)
        * keep[:, None, :, None]
    ).reshape(integrals.shape)
    half_bit = lax.axis_size("row").bit_length() - 2
    ladder = jnp.dot(
        lax.all_gather(amplitudes, "row", axis=0, tiled=True),
        masked,
        preferred_element_type=jnp.float32,
    )
    partner = from_partner(ladder, "row", half_bit)
    partner = partner.reshape(OT, OT, product_count, TS, TS)
    partner = jnp.transpose(partner, (1, 0, 2, 4, 3)).reshape(ladder.shape)
    summed = lax.psum_scatter(ladder + partner, "col", scatter_dimension=0, tiled=True)
    return summed.astype(jnp.bfloat16)


NZ, NX, NY, NC = 4, 2, 2, 2
ROWS = 128
PART = 64
OWNED = 256
WIDTH = 2048
PANELS = WIDTH // TP
LANES = 128
PLANES = ((0, 1, 2, 3), (1, 0, 2, 3), (2, 3, 1, 0), (3, 2, 1, 0))
PART_OF = (1, 2, 0, 3)


def params(mib):
    return pltpu.CompilerParams(vmem_limit_bytes=mib * 2**20)


def light():
    return pl.CostEstimate(flops=1000, bytes_accessed=1000, transcendentals=0)


def selection(extents, axes):
    n = int(np.prod(extents))
    row = lax.broadcasted_iota(jnp.int32, (n, n), 0)
    column = lax.broadcasted_iota(jnp.int32, (n, n), 1)
    strides = [int(np.prod(extents[axis + 1 :])) for axis in range(len(extents))]
    source, below = jnp.zeros_like(row), 1
    for axis in reversed(axes):
        source += row // below % extents[axis] * strides[axis]
        below *= extents[axis]
    return jnp.where(source == column, 1.0, 0.0).astype(jnp.bfloat16)


def block_order():
    return selection((4, 32), (1, 0))


def align_order():
    return selection((2, 2, 4, 4), (1, 0, 3, 2))


def natural_order():
    return selection((4, 2, 8, 4), (1, 3, 0, 2))


def swap_order():
    return selection((TS, TS), (1, 0))


def send(value, target):
    pairs = []
    for n, (z, x, y, k) in enumerate(np.ndindex(NZ, NX, NY, NC)):
        to = target(z, x, y, k)
        if to is not None:
            pairs.append((n, int(np.ravel_multi_index(to, (NZ, NX, NY, NC)))))
    return lax.ppermute(value, ("row", "col"), pairs)


def along_z(value, moves):
    return send(value, lambda z, x, y, k: (moves[z], x, y, k) if z in moves else None)


def across_x(value, planes=range(NZ)):
    return send(value, lambda z, x, y, k: (z, 1 - x, y, k) if z in planes else None)


def across_y(value):
    return send(value, lambda z, x, y, k: (z, x, 1 - y, k))


def across_core(value):
    return send(value, lambda z, x, y, k: (z, x, y, 1 - k))


def to_partner(value):
    return send(value, lambda z, x, y, k: (z ^ 2, x, y, k))


def to_owner(value, steps):
    def target(z, x, y, k):
        owned = [divmod(PLANES[z][step], NC) for step in steps]
        return (z, x, 1 - y, k) if (1 - y, k) in owned else None

    return send(value, target)


def matmul(a, b):
    return jnp.dot(a, b, preferred_element_type=jnp.float32)


def lookup(table, index):
    value = table[0]
    for n in range(1, len(table)):
        value = jnp.where(index == n, table[n], value)
    return value


def ladder_kernel(place, irrep, product, summed, here, beside, integrals, out, rows):
    x, col = place[0] % NX, place[1]
    order = block_order()
    for block, at in ((here, x), (beside, 1 - x)):
        start = pl.multiple_of(at * ROWS, ROWS)
        rows[pl.ds(start, ROWS), :] = matmul(order, block[...]).astype(jnp.bfloat16)
    for p in range(PANELS):
        wanted = irrep[product[p, 0]] ^ irrep[product[p, 1]]
        kept = []
        for q in range(WIDTH // TP):
            same = (irrep[summed[q, 0]] ^ irrep[summed[q, 1]]) == wanted
            value = rows[:, q * TP : (q + 1) * TP]
            kept.append(jnp.where(same, value, jnp.zeros_like(value)))
        cut = slice(p * TP, (p + 1) * TP)
        total = matmul(jnp.concatenate(kept, axis=1), integrals[:, cut])
        for to in range(4):
            for at in range(2):
                start = at * ROWS + to * 32
                out[lookup(PART_OF, to ^ col), at * 32 : (at + 1) * 32, cut] = total[start : start + 32, :]


def partial_ladder(tables, integrals, here, beside):
    vmem = pl.BlockSpec(memory_space=pltpu.VMEM)
    return pl.pallas_call(
        ladder_kernel,
        in_specs=[pl.BlockSpec(memory_space=pltpu.SMEM)] * 4 + [vmem] * 3,
        out_specs=vmem,
        scratch_shapes=[pltpu.VMEM((2 * ROWS, WIDTH), jnp.bfloat16)],
        out_shape=jax.ShapeDtypeStruct((4, PART, WIDTH), jnp.float32),
        compiler_params=params(14),
        cost_estimate=light(),
        name="partial_ladder",
    )(*tables, here, beside, integrals)


def turn(arrived):
    high = arrived.astype(jnp.bfloat16)
    low = (arrived - high.astype(jnp.float32)).astype(jnp.bfloat16)
    both = jnp.concatenate([high, low], axis=0)
    swap, align = swap_order(), align_order()
    cuts = [both[:, p * TP : (p + 1) * TP] for p in range(PANELS)]
    both = jnp.concatenate([matmul(cut, swap).astype(jnp.bfloat16) for cut in cuts], axis=1)
    return matmul(align, both[:PART]) + matmul(align, both[PART:])


def turn_kernel(arrived, out):
    out[...] = turn(decoded(arrived))


def turned(arrived):
    return pl.pallas_call(
        turn_kernel,
        out_shape=jax.ShapeDtypeStruct((PART, WIDTH), jnp.float32),
        compiler_params=params(12),
        cost_estimate=pl.CostEstimate(flops=2 * 10**9, bytes_accessed=10**6, transcendentals=0),
        name="turn",
    )(arrived)


def planes_of(side):
    return [lookup([planes[step] for planes in PLANES], side) for step in range(4)]


def sort_own_kernel(step, place, pair, mine, *refs):
    own, sems = refs[-2:]

    @pl.when(planes_of(place[0] // NX)[step] == place[1])
    def _():
        copies = [
            pltpu.make_async_copy(pair.at[0], own.at[0], sems.at[0]),
            pltpu.make_async_copy(mine, own.at[1], sems.at[1]),
            pltpu.make_async_copy(pair.at[pl.ds(2, 2)], own.at[pl.ds(2, 2)], sems.at[2]),
        ]
        for copy in copies:
            copy.start()
        for copy in copies:
            copy.wait()


def sort_owed_kernel(step, place, pair, *refs):
    owed, buffer, sem = refs[-3:]

    @pl.when(planes_of(place[0] // NX)[step] == place[1] ^ 2)
    def _():
        put_coded(buffer, pair[1:])
        copy = pltpu.make_async_copy(buffer, owed, sem)
        copy.start()
        copy.wait()


def sort(kernel, shape, scratch, place, step, values, before):
    vmem = pl.BlockSpec(memory_space=pltpu.VMEM)
    hbm = pl.BlockSpec(memory_space=pl.ANY)
    before = [] if before is None else [before]
    return pl.pallas_call(
        functools.partial(kernel, step),
        in_specs=[pl.BlockSpec(memory_space=pltpu.SMEM)] + [vmem] * len(values) + [hbm] * len(before),
        out_specs=hbm,
        out_shape=jax.ShapeDtypeStruct(shape, jnp.float32),
        scratch_shapes=scratch,
        input_output_aliases={1 + len(values): 0} if before else {},
        compiler_params=params(10),
        cost_estimate=light(),
        name="sort",
    )(place, *values, *before)


def sort_own(place, step, pair, mine, before=None):
    return sort(sort_own_kernel, (4, PART, WIDTH), [pltpu.SemaphoreType.DMA((3,))], place, step, (pair, mine), before)


def sort_owed(place, step, pair, before=None):
    shape = (3, PART, WIDTH + LANES)
    scratch = [pltpu.VMEM(shape, jnp.float32), pltpu.SemaphoreType.DMA]
    return sort(sort_owed_kernel, shape, scratch, place, step, (pair,), before)


def gather_kernel(place, own, rest, out):
    for part, (distance, came) in enumerate(((2, 0), (0, None), (1, 2), (3, 1))):
        value = own[part]
        if came is not None:
            value += decoded(rest.at[came])
        out[distance ^ place[1]] = value


def merge_kernel(place, sums, turned0, turned1, turned2, out):
    out[...] = sums[...]
    for step, ref in enumerate((turned0, turned1, turned2)):
        plane = planes_of(place[0] // NX ^ 2)[step]
        out[plane] = out[plane] + ref[...]


def gather(kernel, place, *values):
    vmem = pl.BlockSpec(memory_space=pltpu.VMEM)
    return pl.pallas_call(
        kernel,
        in_specs=[pl.BlockSpec(memory_space=pltpu.SMEM)] + [vmem] * len(values),
        out_specs=vmem,
        out_shape=jax.ShapeDtypeStruct((4, PART, WIDTH), jnp.float32),
        compiler_params=params(12),
        cost_estimate=light(),
        name="gather",
    )(place, *values)


def finish_kernel(place, sums, last, out, total):
    total[...] = sums[...].astype(jnp.bfloat16)
    plane = planes_of(place[0] // NX ^ 2)[3]
    total[plane] = (sums[plane] + turn(decoded(last))).astype(jnp.bfloat16)
    natural = natural_order()
    value = total[...].reshape(OWNED, WIDTH)
    for p in range(PANELS):
        cut = slice(p * TP, (p + 1) * TP)
        out[:, cut] = matmul(natural, value[:, cut]).astype(jnp.bfloat16)


def finish(place, sums, last):
    vmem = pl.BlockSpec(memory_space=pltpu.VMEM)
    return pl.pallas_call(
        finish_kernel,
        in_specs=[pl.BlockSpec(memory_space=pltpu.SMEM), vmem, vmem],
        out_specs=vmem,
        out_shape=jax.ShapeDtypeStruct((OWNED, WIDTH), jnp.bfloat16),
        scratch_shapes=[pltpu.VMEM((4, PART, WIDTH), jnp.bfloat16)],
        compiler_params=params(12),
        cost_estimate=light(),
        name="finish",
    )(place, sums, last)


def coded(value):
    largest = value
    while largest.ndim > 0 and largest.shape != (1,) * value.ndim:
        axis = next(n for n, size in enumerate(largest.shape) if size > 1)
        largest = jnp.max(jnp.abs(largest), axis=axis, keepdims=True)
    power = jnp.ceil(jnp.log2(jnp.maximum(largest, 1e-30)))
    scaled = value * jnp.exp2(7 - power)
    return scaled * jnp.abs(scaled), jnp.broadcast_to(power, (*value.shape[:-1], LANES))


def put_coded(ref, value):
    ref[..., :WIDTH], ref[..., WIDTH:] = coded(value)


def decoded(ref):
    value = ref[..., :WIDTH]
    power = ref[..., WIDTH : WIDTH + 1]
    root = jnp.sqrt(jnp.abs(value)) * jnp.exp2(power - 7)
    return jnp.where(value < 0, -root, root)


def wire(value):
    return value.astype(WIRE)


def unwire(value):
    return value.astype(jnp.float32)


def small_kernel(kernel, shapes, mib, name):
    vmem = pl.BlockSpec(memory_space=pltpu.VMEM)
    shapes = [jax.ShapeDtypeStruct(shape, jnp.float32) for shape in shapes]
    return pl.pallas_call(
        kernel,
        out_specs=[vmem] * len(shapes),
        out_shape=shapes,
        compiler_params=params(mib),
        cost_estimate=light(),
        name=name,
    )


def add_cores_kernel(part, sibling, pair, out):
    for n in (0, 1, 2, 3):
        pair[n] = part[n] + sibling[3 - n]
    put_coded(out, pair[0])


def add_cores(part):
    call = small_kernel(add_cores_kernel, [(4, PART, WIDTH), (PART, WIDTH + LANES)], 12, "add_cores")
    return call(part, across_core(part))


def add_chips_kernel(pair, over, mine, out):
    mine[...] = pair[1] + decoded(over)
    put_coded(out, mine[...])


def add_chips(pair, over):
    call = small_kernel(add_chips_kernel, [(PART, WIDTH), (PART, WIDTH + LANES)], 8, "add_chips")
    return call(pair, unwire(over))


def together(*values):
    return lax.optimization_barrier(values)


def on_device(amplitudes, integrals, tile_irrep, product_pairs, summed_pairs):
    row, col = lax.axis_index("row"), lax.axis_index("col")
    z = row // NX
    place = jnp.stack([row, col]).astype(jnp.int32)
    tables = (place, tile_irrep, product_pairs, summed_pairs)
    inner = (z == 1) | (z == 2)
    outward = {0: 1, 1: 0, 2: 3, 3: 2}
    inward = {1: 2, 2: 1}

    here0 = amplitudes
    beside0 = across_x(here0)
    here1 = along_z(here0, outward)
    middle = along_z(here0, inward)
    beside0, here1, middle = together(beside0, here1, middle)

    beside1 = across_x(here1)
    crossed = along_z(here1, inward)
    here2 = along_z(middle, outward)
    part0 = partial_ladder(tables, integrals, here0, beside0)
    beside1, crossed, here2, part0 = together(beside1, crossed, here2, part0)
    here2 = jnp.where(inner, middle, here2)

    beside2 = across_x(here2)
    here3 = along_z(crossed, outward)
    pair0, sent = add_cores(part0)
    over0 = across_y(wire(sent))
    part1 = partial_ladder(tables, integrals, here1, beside1)
    owed02 = sort_owed(place, 0, pair0)
    beside2, here3, pair0, over0, part1, owed02 = together(beside2, here3, pair0, over0, part1, owed02)
    here3 = jnp.where(inner, crossed, here3)

    beside3 = across_x(here3)
    mine0, sent = add_chips(pair0, over0)
    other0 = to_partner(wire(sent))
    pair1, sent = add_cores(part1)
    over1 = across_y(wire(sent))
    part2 = partial_ladder(tables, integrals, here2, beside2)
    own = sort_own(place, 0, pair0, mine0)
    owed13 = sort_owed(place, 1, pair1)
    beside3, other0, own, owed02, owed13, pair1, over1, part2 = together(
        beside3, other0, own, owed02, owed13, pair1, over1, part2
    )

    mine1, sent = add_chips(pair1, over1)
    other1 = to_partner(wire(sent))
    pair2, sent = add_cores(part2)
    over2 = across_y(wire(sent))
    part3 = partial_ladder(tables, integrals, here3, beside3)
    own = sort_own(place, 1, pair1, mine1, own)
    owed02 = wire(sort_owed(place, 2, pair2, owed02))
    other0, other1, own, owed02, owed13, pair2, over2, part3 = together(
        other0, other1, own, owed02, owed13, pair2, over2, part3
    )

    mine2, sent = add_chips(pair2, over2)
    sent, owed02 = together(wire(sent), owed02)
    other2 = to_partner(sent)
    came02 = to_owner(owed02, (0, 2))
    pair3, sent = add_cores(part3)
    over3 = across_y(wire(sent))
    own = sort_own(place, 2, pair2, mine2, own)
    owed13 = wire(sort_owed(place, 3, pair3, owed13))
    other0, other1, other2, own, came02, owed13, pair3, over3 = together(
        other0, other1, other2, own, came02, owed13, pair3, over3
    )

    mine3, sent = add_chips(pair3, over3)
    sent, other0, other1, other2 = together(sent, other0, other1, other2)
    other3 = to_partner(wire(sent))
    came13 = to_owner(owed13, (1, 3))
    own = sort_own(place, 3, pair3, mine3, own)
    done = [turned(unwire(other)) for other in (other0, other1, other2)]
    sums = gather(gather_kernel, place, own, unwire(came02 + came13))
    sums = gather(merge_kernel, place, sums, *done)
    return finish(place, sums, unwire(other3))


def solution(mesh):
    body = on_device if (mesh.shape["row"], mesh.shape["col"]) == (NZ * NX, NY * NC) else plain
    return jax.shard_map(
        body,
        mesh=mesh,
        in_specs=(P("row", "col"), P("col", "row"), P(), P("row", None), P("col", None)),
        out_specs=P("col", "row"),
        check_vma=False,
    )
```

```python
import functools

import jax
import jax.numpy as jnp
import numpy as np
from jax import lax
from jax.experimental import pallas as pl
from jax.experimental.pallas import tpu as pltpu
from jax.sharding import PartitionSpec as P

TS = 16
TP = TS * TS
OT = 32
WIRE = jnp.float16


def from_partner(value, axis, distance):
    mask = 2**distance
    pairs = [(source, source ^ mask) for source in range(lax.axis_size(axis))]
    return lax.ppermute(value, axis, pairs)


def pair_symmetry(tile_irrep, pairs):
    return jnp.bitwise_xor(tile_irrep[pairs[:, 0]], tile_irrep[pairs[:, 1]])


def plain(amplitudes, integrals, tile_irrep, product_pairs, summed_pairs):
    product_sym = pair_symmetry(tile_irrep, product_pairs)
    summed_sym = pair_symmetry(tile_irrep, summed_pairs)
    allowed = summed_sym[:, None] == product_sym[None, :]
    summed_count = summed_pairs.shape[0]
    product_count = product_pairs.shape[0]
    keep = allowed.astype(integrals.dtype)
    masked = (
        integrals.reshape(summed_count, TP, product_count, TP)
        * keep[:, None, :, None]
    ).reshape(integrals.shape)
    half_bit = lax.axis_size("row").bit_length() - 2
    ladder = jnp.dot(
        lax.all_gather(amplitudes, "row", axis=0, tiled=True),
        masked,
        preferred_element_type=jnp.float32,
    )
    partner = from_partner(ladder, "row", half_bit)
    partner = partner.reshape(OT, OT, product_count, TS, TS)
    partner = jnp.transpose(partner, (1, 0, 2, 4, 3)).reshape(ladder.shape)
    summed = lax.psum_scatter(ladder + partner, "col", scatter_dimension=0, tiled=True)
    return summed.astype(jnp.bfloat16)


NZ, NX, NY, NC = 4, 2, 2, 2
ROWS = 128
HALF = 32
PART = 2 * HALF
OWNED = 256
WIDTH = 2048
PANELS = WIDTH // TP
LANES = 128
PLANES = ((0, 1, 2, 3), (1, 0, 2, 3), (2, 3, 1, 0), (3, 2, 1, 0))
PART_OF = (1, 2, 0, 3)


CHUNKS = (((0, 0),), ((0, 1), (1, 0)), ((1, 1), (2, 0)), ((2, 1), (3, 0)), ((3, 1),))


def params(mib):
    return pltpu.CompilerParams(vmem_limit_bytes=mib * 2**20)


def light():
    return pl.CostEstimate(flops=1000, bytes_accessed=1000, transcendentals=0)


def selection(extents, axes):
    n = int(np.prod(extents))
    row = lax.broadcasted_iota(jnp.int32, (n, n), 0)
    column = lax.broadcasted_iota(jnp.int32, (n, n), 1)
    strides = [int(np.prod(extents[axis + 1 :])) for axis in range(len(extents))]
    source, below = jnp.zeros_like(row), 1
    for axis in reversed(axes):
        source += row // below % extents[axis] * strides[axis]
        below *= extents[axis]
    return jnp.where(source == column, 1.0, 0.0).astype(jnp.bfloat16)


def block_order():
    return selection((4, 32), (1, 0))


def align_order():
    return selection((2, 4, 4), (0, 2, 1))


def natural_order():
    return selection((4, 2, 8, 4), (1, 3, 0, 2))


def swap_order():
    return selection((TS, TS), (1, 0))


def send(value, target):
    pairs = []
    for n, (z, x, y, k) in enumerate(np.ndindex(NZ, NX, NY, NC)):
        to = target(z, x, y, k)
        if to is not None:
            pairs.append((n, int(np.ravel_multi_index(to, (NZ, NX, NY, NC)))))
    return lax.ppermute(value, ("row", "col"), pairs)


def along_z(value, moves):
    return send(value, lambda z, x, y, k: (moves[z], x, y, k) if z in moves else None)


def across_x(value, planes=range(NZ)):
    return send(value, lambda z, x, y, k: (z, 1 - x, y, k) if z in planes else None)


def across_y(value):
    return send(value, lambda z, x, y, k: (z, x, 1 - y, k))


def across_core(value):
    return send(value, lambda z, x, y, k: (z, x, y, 1 - k))


def to_partner(value):
    return send(value, lambda z, x, y, k: (z ^ 2, x, y, k))


def matmul(a, b):
    return jnp.dot(a, b, preferred_element_type=jnp.float32)


def lookup(table, index):
    value = table[0]
    for n in range(1, len(table)):
        value = jnp.where(index == n, table[n], value)
    return value


def ladder_kernel(place, irrep, product, summed, *refs):
    blocks, (integrals, out, rows) = refs[:-3], refs[-3:]
    order = block_order()
    for n, block in enumerate(blocks):
        rows[n * ROWS : (n + 1) * ROWS, :] = matmul(order, block[...]).astype(jnp.bfloat16)
    for p in range(PANELS):
        wanted = irrep[product[p, 0]] ^ irrep[product[p, 1]]
        kept = []
        for q in range(WIDTH // TP):
            same = (irrep[summed[q, 0]] ^ irrep[summed[q, 1]]) == wanted
            value = rows[:, q * TP : (q + 1) * TP]
            kept.append(jnp.where(same, value, jnp.zeros_like(value)))
        cut = slice(p * TP, (p + 1) * TP)
        total = matmul(jnp.concatenate(kept, axis=1), integrals[:, cut])
        for to in range(4):
            for n in range(len(blocks)):
                start = n * ROWS + to * HALF
                out[lookup(PART_OF, to ^ place[1]), n * HALF : (n + 1) * HALF, cut] = total[start : start + HALF, :]


def partial_ladder(tables, integrals, *blocks):
    vmem = pl.BlockSpec(memory_space=pltpu.VMEM)
    return pl.pallas_call(
        ladder_kernel,
        in_specs=[pl.BlockSpec(memory_space=pltpu.SMEM)] * 4 + [vmem] * (len(blocks) + 1),
        out_specs=vmem,
        scratch_shapes=[pltpu.VMEM((len(blocks) * ROWS, WIDTH), jnp.bfloat16)],
        out_shape=jax.ShapeDtypeStruct((4, len(blocks) * HALF, WIDTH), jnp.float32),
        compiler_params=params(14),
        cost_estimate=light(),
        name="partial_ladder",
    )(*tables, *blocks, integrals)


def turn(arrived):
    high = arrived.astype(jnp.bfloat16)
    low = (arrived - high.astype(jnp.float32)).astype(jnp.bfloat16)
    both = jnp.concatenate([high, low], axis=0)
    swap, align = swap_order(), align_order()
    cuts = [both[:, p * TP : (p + 1) * TP] for p in range(PANELS)]
    both = jnp.concatenate([matmul(cut, swap).astype(jnp.bfloat16) for cut in cuts], axis=1)
    halves = [matmul(align, both[n : n + HALF]) for n in range(0, both.shape[0], HALF)]
    count = len(halves) // 2
    return jnp.concatenate([high + low for high, low in zip(halves[:count], halves[count:], strict=True)], axis=0)


def turn_kernel(arrived, out):
    out[...] = turn(decoded(arrived))


def turned(arrived):
    return pl.pallas_call(
        turn_kernel,
        out_shape=jax.ShapeDtypeStruct((arrived.shape[0], WIDTH), jnp.float32),
        compiler_params=params(12),
        cost_estimate=pl.CostEstimate(flops=2 * 10**9, bytes_accessed=10**6, transcendentals=0),
        name="turn",
    )(arrived)


def planes_of(side):
    return [lookup([planes[step] for planes in PLANES], side) for step in range(4)]


def sort_own_kernel(steps, place, pair, mine, *refs):
    own, sems = refs[-2:]
    for n, (step, across) in enumerate(steps):

        @pl.when(planes_of(place[0] // NX)[step] == place[1])
        def _(n=n, across=across):
            rows = pl.ds(n * HALF, HALF)
            to = pl.ds(pl.multiple_of((place[0] % NX ^ across) * HALF, HALF), HALF)
            copies = [
                pltpu.make_async_copy(pair.at[0, rows], own.at[0, to], sems.at[0]),
                pltpu.make_async_copy(mine.at[rows], own.at[1, to], sems.at[1]),
                pltpu.make_async_copy(pair.at[pl.ds(2, 2), rows], own.at[pl.ds(2, 2), to], sems.at[2]),
            ]
            for copy in copies:
                copy.start()
            for copy in copies:
                copy.wait()


def sort_owed_kernel(steps, place, pair, *refs):
    owed, buffer, sem = refs[-3:]
    ((n, step),) = steps

    @pl.when(planes_of(place[0] // NX)[step] == place[1] ^ 2)
    def _():
        put_coded(buffer, pair[1:, n * HALF : (n + 1) * HALF])
        copy = pltpu.make_async_copy(buffer, owed, sem)
        copy.start()
        copy.wait()


def sort(kernel, shape, scratch, place, steps, values, before):
    vmem = pl.BlockSpec(memory_space=pltpu.VMEM)
    hbm = pl.BlockSpec(memory_space=pl.ANY)
    before = [] if before is None else [before]
    return pl.pallas_call(
        functools.partial(kernel, steps),
        in_specs=[pl.BlockSpec(memory_space=pltpu.SMEM)] + [vmem] * len(values) + [hbm] * len(before),
        out_specs=hbm,
        out_shape=jax.ShapeDtypeStruct(shape, jnp.float32),
        scratch_shapes=scratch,
        input_output_aliases={1 + len(values): 0} if before else {},
        compiler_params=params(10),
        cost_estimate=light(),
        name="sort",
    )(place, *values, *before)


def sort_own(place, steps, pair, mine, before=None):
    return sort(sort_own_kernel, (4, PART, WIDTH), [pltpu.SemaphoreType.DMA((3,))], place, steps, (pair, mine), before)


def sort_owed(place, step, pair, before=None, across=0):
    n = next(n for chunk in CHUNKS for n, block in enumerate(chunk) if block == (step, across))
    scratch = [pltpu.VMEM((3, HALF, WIDTH + LANES), jnp.float32), pltpu.SemaphoreType.DMA]
    return sort(sort_owed_kernel, (3, HALF, WIDTH + LANES), scratch, place, ((n, step),), (pair,), before)


def place_rest(place, ref, rest, across):
    rows = pl.ds(pl.multiple_of((place[0] % NX ^ across) * HALF, HALF), HALF)
    for came, distance in enumerate((0, 1, 3)):
        ref[distance ^ 2 ^ place[1], rows, :] += decoded(rest.at[came])


def places(place, step, across):
    x = place[0] % NX ^ across
    plane = planes_of(place[0] // NX ^ 2)[step]
    return plane, [pl.ds(pl.multiple_of(to * HALF + x * 16, 16), 16) for to in range(NX)]


def gather_kernel(place, own, rest, *refs):
    out = refs[-1]
    for part, distance in enumerate((2, 0, 1, 3)):
        out[distance ^ place[1]] = own[part]
    place_rest(place, out, rest, 0)
    for steps, ref in zip(CHUNKS, refs[:-1]):
        for n, (step, across) in enumerate(steps):
            plane, rows = places(place, step, across)
            for to in range(NX):
                out[plane, rows[to], :] += ref[pl.ds(n * HALF + to * 16, 16), :]


def gather(place, own, rest, done):
    vmem = pl.BlockSpec(memory_space=pltpu.VMEM)
    return pl.pallas_call(
        gather_kernel,
        in_specs=[pl.BlockSpec(memory_space=pltpu.SMEM)] + [vmem] * (2 + len(done)),
        out_specs=vmem,
        out_shape=jax.ShapeDtypeStruct((4, PART, WIDTH), jnp.float32),
        compiler_params=params(14),
        cost_estimate=light(),
        name="gather",
    )(place, own, rest, *done)


def finish_kernel(place, sums, rest, last, out, all_sums, total):
    all_sums[...] = sums[...]
    place_rest(place, all_sums, rest, 1)
    value = turn(decoded(last))
    for n, (step, across) in enumerate(CHUNKS[-1]):
        plane, rows = places(place, step, across)
        for to in range(NX):
            start = n * HALF + to * 16
            all_sums[plane, rows[to], :] += value[start : start + 16]
    total[...] = all_sums[...].astype(jnp.bfloat16)
    natural = natural_order()
    value = total[...].reshape(OWNED, WIDTH)
    for p in range(PANELS):
        cut = slice(p * TP, (p + 1) * TP)
        out[:, cut] = matmul(natural, value[:, cut]).astype(jnp.bfloat16)


def finish(place, sums, rest, last):
    vmem = pl.BlockSpec(memory_space=pltpu.VMEM)
    return pl.pallas_call(
        finish_kernel,
        in_specs=[pl.BlockSpec(memory_space=pltpu.SMEM), vmem, vmem, vmem],
        out_specs=vmem,
        out_shape=jax.ShapeDtypeStruct((OWNED, WIDTH), jnp.bfloat16),
        scratch_shapes=[pltpu.VMEM((4, PART, WIDTH), jnp.float32), pltpu.VMEM((4, PART, WIDTH), jnp.bfloat16)],
        compiler_params=params(14),
        cost_estimate=light(),
        name="finish",
    )(place, sums, rest, last)


def coded(value):
    largest = value
    while largest.ndim > 0 and largest.shape != (1,) * value.ndim:
        axis = next(n for n, size in enumerate(largest.shape) if size > 1)
        largest = jnp.max(jnp.abs(largest), axis=axis, keepdims=True)
    power = jnp.ceil(jnp.log2(jnp.maximum(largest, 1e-30)))
    scaled = value * jnp.exp2(7 - power)
    return scaled * jnp.abs(scaled), jnp.broadcast_to(power, (*value.shape[:-1], LANES))


def put_coded(ref, value):
    ref[..., :WIDTH], ref[..., WIDTH:] = coded(value)


def decoded(ref):
    value = ref[..., :WIDTH]
    power = ref[..., WIDTH : WIDTH + 1]
    root = jnp.sqrt(jnp.abs(value)) * jnp.exp2(power - 7)
    return jnp.where(value < 0, -root, root)


def wire(value):
    return value.astype(WIRE)


def unwire(value):
    return value.astype(jnp.float32)


def small_kernel(kernel, shapes, mib, name):
    vmem = pl.BlockSpec(memory_space=pltpu.VMEM)
    shapes = [jax.ShapeDtypeStruct(shape, jnp.float32) for shape in shapes]
    return pl.pallas_call(
        kernel,
        out_specs=[vmem] * len(shapes),
        out_shape=shapes,
        compiler_params=params(mib),
        cost_estimate=light(),
        name=name,
    )


def add_cores_kernel(part, sibling, pair, out):
    for n in (0, 1, 2, 3):
        pair[n] = part[n] + sibling[3 - n]
    put_coded(out, pair[0])


def add_cores(part):
    call = small_kernel(add_cores_kernel, [part.shape, (part.shape[1], WIDTH + LANES)], 12, "add_cores")
    return call(part, across_core(part))


def add_chips_kernel(pair, over, mine, out):
    mine[...] = pair[1] + decoded(over)
    put_coded(out, mine[...])


def add_chips(pair, over):
    call = small_kernel(add_chips_kernel, [pair.shape[1:], over.shape], 8, "add_chips")
    return call(pair, unwire(over))


def together(*values):
    return lax.optimization_barrier(values)


def on_device(amplitudes, integrals, tile_irrep, product_pairs, summed_pairs):
    row, col = lax.axis_index("row"), lax.axis_index("col")
    z = row // NX
    place = jnp.stack([row, col]).astype(jnp.int32)
    tables = (place, tile_irrep, product_pairs, summed_pairs)
    inner = (z == 1) | (z == 2)
    outward = {0: 1, 1: 0, 2: 3, 3: 2}
    inward = {1: 2, 2: 1}

    here0 = amplitudes
    beside0 = across_x(here0)
    here1 = along_z(here0, outward)
    middle = along_z(here0, inward)
    part0 = partial_ladder(tables, integrals, here0)
    beside0, here1, middle, part0 = together(beside0, here1, middle, part0)

    beside1 = across_x(here1)
    crossed = along_z(here1, inward)
    here2 = along_z(middle, outward)
    pair0, sent = add_cores(part0)
    over0 = across_y(wire(sent))
    part1 = partial_ladder(tables, integrals, beside0, here1)
    beside1, crossed, here2, pair0, over0, part1 = together(beside1, crossed, here2, pair0, over0, part1)
    here2 = jnp.where(inner, middle, here2)

    beside2 = across_x(here2)
    here3 = along_z(crossed, outward)
    mine0, sent = add_chips(pair0, over0)
    other0 = to_partner(wire(sent))
    pair1, sent = add_cores(part1)
    over1 = across_y(wire(sent))
    part2 = partial_ladder(tables, integrals, beside1, here2)
    own = sort_own(place, CHUNKS[0], pair0, mine0)
    owed_here = sort_owed(place, 0, pair0)
    beside2, here3, other0, own, owed_here, pair1, over1, part2 = together(
        beside2, here3, other0, own, owed_here, pair1, over1, part2
    )
    here3 = jnp.where(inner, crossed, here3)

    beside3 = across_x(here3)
    mine1, sent = add_chips(pair1, over1)
    other1 = to_partner(wire(sent))
    pair2, sent = add_cores(part2)
    over2 = across_y(wire(sent))
    part3 = partial_ladder(tables, integrals, beside2, here3)
    own = sort_own(place, CHUNKS[1], pair1, mine1, own)
    owed_beside = sort_owed(place, 0, pair1, across=1)
    owed_here = sort_owed(place, 1, pair1, owed_here)
    beside3, other0, other1, own, owed_here, owed_beside, pair2, over2, part3 = together(
        beside3, other0, other1, own, owed_here, owed_beside, pair2, over2, part3
    )

    mine2, sent = add_chips(pair2, over2)
    other2 = to_partner(wire(sent))
    pair3, sent = add_cores(part3)
    over3 = across_y(wire(sent))
    part4 = partial_ladder(tables, integrals, beside3)
    own = sort_own(place, CHUNKS[2], pair2, mine2, own)
    owed_beside = sort_owed(place, 1, pair2, owed_beside, across=1)
    owed_here = sort_owed(place, 2, pair2, owed_here)
    owed_beside = sort_owed(place, 2, pair3, owed_beside, across=1)
    owed_here = wire(sort_owed(place, 3, pair3, owed_here))
    other0, other1, other2, own, owed_here, owed_beside, pair3, over3, part4 = together(
        other0, other1, other2, own, owed_here, owed_beside, pair3, over3, part4
    )

    mine3, sent = add_chips(pair3, over3)
    sent, owed_here = together(wire(sent), owed_here)
    other3 = to_partner(sent)
    came_here = across_y(owed_here)
    pair4, sent = add_cores(part4)
    over4 = across_y(wire(sent))
    own = sort_own(place, CHUNKS[3], pair3, mine3, own)
    owed_beside = wire(sort_owed(place, 3, pair4, owed_beside, across=1))
    other0, other1, other2, other3, own, came_here, pair4, over4 = together(
        other0, other1, other2, other3, own, came_here, pair4, over4
    )

    mine4, sent = add_chips(pair4, over4)
    sent, *others = together(sent, other0, other1, other2, other3)
    other4 = to_partner(wire(sent))
    came_beside = across_y(owed_beside)
    own = sort_own(place, CHUNKS[4], pair4, mine4, own)
    done = [turned(unwire(other)) for other in others]
    sums = gather(place, own, unwire(came_here), done)
    return finish(place, sums, unwire(came_beside), unwire(other4))


def solution(mesh):
    body = on_device if (mesh.shape["row"], mesh.shape["col"]) == (NZ * NX, NY * NC) else plain
    return jax.shard_map(
        body,
        mesh=mesh,
        in_specs=(P("row", "col"), P("col", "row"), P(), P("row", None), P("col", None)),
        out_specs=P("col", "row"),
        check_vma=False,
    )
```

```python
import functools

import jax
import jax.numpy as jnp
import numpy as np
from jax import lax
from jax.experimental import pallas as pl
from jax.experimental.pallas import tpu as pltpu
from jax.sharding import PartitionSpec as P

TS = 16
TP = TS * TS
OT = 32
WIRE = jnp.float16


def from_partner(value, axis, distance):
    mask = 2**distance
    pairs = [(source, source ^ mask) for source in range(lax.axis_size(axis))]
    return lax.ppermute(value, axis, pairs)


def pair_symmetry(tile_irrep, pairs):
    return jnp.bitwise_xor(tile_irrep[pairs[:, 0]], tile_irrep[pairs[:, 1]])


def plain(amplitudes, integrals, tile_irrep, product_pairs, summed_pairs):
    product_sym = pair_symmetry(tile_irrep, product_pairs)
    summed_sym = pair_symmetry(tile_irrep, summed_pairs)
    allowed = summed_sym[:, None] == product_sym[None, :]
    summed_count = summed_pairs.shape[0]
    product_count = product_pairs.shape[0]
    keep = allowed.astype(integrals.dtype)
    masked = (
        integrals.reshape(summed_count, TP, product_count, TP)
        * keep[:, None, :, None]
    ).reshape(integrals.shape)
    half_bit = lax.axis_size("row").bit_length() - 2
    ladder = jnp.dot(
        lax.all_gather(amplitudes, "row", axis=0, tiled=True),
        masked,
        preferred_element_type=jnp.float32,
    )
    partner = from_partner(ladder, "row", half_bit)
    partner = partner.reshape(OT, OT, product_count, TS, TS)
    partner = jnp.transpose(partner, (1, 0, 2, 4, 3)).reshape(ladder.shape)
    summed = lax.psum_scatter(ladder + partner, "col", scatter_dimension=0, tiled=True)
    return summed.astype(jnp.bfloat16)


NZ, NX, NY, NC = 4, 2, 2, 2
ROWS = 128
HALF = 32
PART = 2 * HALF
OWNED = 256
WIDTH = 2048
PANELS = WIDTH // TP
LANES = 128
PLANES = ((0, 1, 2, 3), (1, 0, 2, 3), (2, 3, 1, 0), (3, 2, 1, 0))
PART_OF = (1, 2, 0, 3)


CHUNKS = (((0, 0),), ((0, 1), (1, 0)), ((1, 1), (2, 0)), ((2, 1), (3, 0)), ((3, 1),))


def params(mib):
    return pltpu.CompilerParams(vmem_limit_bytes=mib * 2**20)


def light():
    return pl.CostEstimate(flops=1000, bytes_accessed=1000, transcendentals=0)


def selection(extents, axes):
    n = int(np.prod(extents))
    row = lax.broadcasted_iota(jnp.int32, (n, n), 0)
    column = lax.broadcasted_iota(jnp.int32, (n, n), 1)
    strides = [int(np.prod(extents[axis + 1 :])) for axis in range(len(extents))]
    source, below = jnp.zeros_like(row), 1
    for axis in reversed(axes):
        source += row // below % extents[axis] * strides[axis]
        below *= extents[axis]
    return jnp.where(source == column, 1.0, 0.0).astype(jnp.bfloat16)


def block_order():
    return selection((4, 32), (1, 0))


def align_order():
    return selection((2, 4, 4), (0, 2, 1))


def natural_order():
    return selection((4, 2, 8, 4), (1, 3, 0, 2))


def swap_order():
    return selection((TS, TS), (1, 0))


def send(value, target):
    pairs = []
    for n, (z, x, y, k) in enumerate(np.ndindex(NZ, NX, NY, NC)):
        to = target(z, x, y, k)
        if to is not None:
            pairs.append((n, int(np.ravel_multi_index(to, (NZ, NX, NY, NC)))))
    return lax.ppermute(value, ("row", "col"), pairs)


def along_z(value, moves):
    return send(value, lambda z, x, y, k: (moves[z], x, y, k) if z in moves else None)


def across_x(value, planes=range(NZ)):
    return send(value, lambda z, x, y, k: (z, 1 - x, y, k) if z in planes else None)


def across_y(value):
    return send(value, lambda z, x, y, k: (z, x, 1 - y, k))


def across_core(value):
    return send(value, lambda z, x, y, k: (z, x, y, 1 - k))


def to_partner(value):
    return send(value, lambda z, x, y, k: (z ^ 2, x, y, k))


def matmul(a, b):
    return jnp.dot(a, b, preferred_element_type=jnp.float32)


def lookup(table, index):
    value = table[0]
    for n in range(1, len(table)):
        value = jnp.where(index == n, table[n], value)
    return value


def ladder_kernel(place, irrep, product, summed, *refs):
    blocks, (integrals, out, rows) = refs[:-3], refs[-3:]
    order = block_order()
    for n, block in enumerate(blocks):
        rows[n * ROWS : (n + 1) * ROWS, :] = matmul(order, block[...]).astype(jnp.bfloat16)
    for p in range(PANELS):
        wanted = irrep[product[p, 0]] ^ irrep[product[p, 1]]
        kept = []
        for q in range(WIDTH // TP):
            same = (irrep[summed[q, 0]] ^ irrep[summed[q, 1]]) == wanted
            value = rows[:, q * TP : (q + 1) * TP]
            kept.append(jnp.where(same, value, jnp.zeros_like(value)))
        cut = slice(p * TP, (p + 1) * TP)
        total = matmul(jnp.concatenate(kept, axis=1), integrals[:, cut])
        for to in range(4):
            for n in range(len(blocks)):
                start = n * ROWS + to * HALF
                out[lookup(PART_OF, to ^ place[1]), n * HALF : (n + 1) * HALF, cut] = total[start : start + HALF, :]


def partial_ladder(tables, integrals, *blocks):
    vmem = pl.BlockSpec(memory_space=pltpu.VMEM)
    return pl.pallas_call(
        ladder_kernel,
        in_specs=[pl.BlockSpec(memory_space=pltpu.SMEM)] * 4 + [vmem] * (len(blocks) + 1),
        out_specs=vmem,
        scratch_shapes=[pltpu.VMEM((len(blocks) * ROWS, WIDTH), jnp.bfloat16)],
        out_shape=jax.ShapeDtypeStruct((4, len(blocks) * HALF, WIDTH), jnp.float32),
        compiler_params=params(14),
        cost_estimate=light(),
        name="partial_ladder",
    )(*tables, *blocks, integrals)


def turn(arrived):
    high = arrived.astype(jnp.bfloat16)
    low = (arrived - high.astype(jnp.float32)).astype(jnp.bfloat16)
    both = jnp.concatenate([high, low], axis=0)
    swap, align = swap_order(), align_order()
    cuts = [both[:, p * TP : (p + 1) * TP] for p in range(PANELS)]
    both = jnp.concatenate([matmul(cut, swap).astype(jnp.bfloat16) for cut in cuts], axis=1)
    halves = [matmul(align, both[n : n + HALF]) for n in range(0, both.shape[0], HALF)]
    count = len(halves) // 2
    return jnp.concatenate([high + low for high, low in zip(halves[:count], halves[count:], strict=True)], axis=0)


def turn_kernel(arrived, out):
    out[...] = turn(decoded(arrived))


def turned(arrived):
    return pl.pallas_call(
        turn_kernel,
        out_shape=jax.ShapeDtypeStruct((arrived.shape[0], WIDTH), jnp.float32),
        compiler_params=params(12),
        cost_estimate=pl.CostEstimate(flops=8 * 10**8, bytes_accessed=10**6, transcendentals=0),
        name="turn",
    )(arrived)


def planes_of(side):
    return [lookup([planes[step] for planes in PLANES], side) for step in range(4)]


def sort_own_kernel(steps, place, pair, mine, *refs):
    own, sems = refs[-2:]
    for n, (step, across) in enumerate(steps):

        @pl.when(planes_of(place[0] // NX)[step] == place[1])
        def _(n=n, across=across):
            rows = pl.ds(n * HALF, HALF)
            to = pl.ds(pl.multiple_of((place[0] % NX ^ across) * HALF, HALF), HALF)
            copies = [
                pltpu.make_async_copy(pair.at[0, rows], own.at[0, to], sems.at[0]),
                pltpu.make_async_copy(mine.at[rows], own.at[1, to], sems.at[1]),
                pltpu.make_async_copy(pair.at[pl.ds(2, 2), rows], own.at[pl.ds(2, 2), to], sems.at[2]),
            ]
            for copy in copies:
                copy.start()
            for copy in copies:
                copy.wait()


def sort_owed_kernel(steps, place, pair, *refs):
    owed, buffer, sem = refs[-3:]
    ((n, step),) = steps

    @pl.when(planes_of(place[0] // NX)[step] == place[1] ^ 2)
    def _():
        put_coded(buffer, pair[1:, n * HALF : (n + 1) * HALF])
        copy = pltpu.make_async_copy(buffer, owed, sem)
        copy.start()
        copy.wait()


def sort(kernel, shape, scratch, place, steps, values, before):
    vmem = pl.BlockSpec(memory_space=pltpu.VMEM)
    hbm = pl.BlockSpec(memory_space=pl.ANY)
    before = [] if before is None else [before]
    return pl.pallas_call(
        functools.partial(kernel, steps),
        in_specs=[pl.BlockSpec(memory_space=pltpu.SMEM)] + [vmem] * len(values) + [hbm] * len(before),
        out_specs=hbm,
        out_shape=jax.ShapeDtypeStruct(shape, jnp.float32),
        scratch_shapes=scratch,
        input_output_aliases={1 + len(values): 0} if before else {},
        compiler_params=params(10),
        cost_estimate=light(),
        name="sort",
    )(place, *values, *before)


def sort_own(place, steps, pair, mine, before=None):
    return sort(sort_own_kernel, (4, PART, WIDTH), [pltpu.SemaphoreType.DMA((3,))], place, steps, (pair, mine), before)


def sort_owed(place, step, pair, before=None, across=0):
    n = next(n for chunk in CHUNKS for n, block in enumerate(chunk) if block == (step, across))
    scratch = [pltpu.VMEM((3, HALF, WIDTH + LANES), jnp.float32), pltpu.SemaphoreType.DMA]
    return sort(sort_owed_kernel, (3, HALF, WIDTH + LANES), scratch, place, ((n, step),), (pair,), before)


def place_rest(place, ref, rest, across):
    rows = pl.ds(pl.multiple_of((place[0] % NX ^ across) * HALF, HALF), HALF)
    for came, distance in enumerate((0, 1, 3)):
        ref[distance ^ 2 ^ place[1], rows, :] += decoded(rest.at[came])


def places(place, step, across):
    x = place[0] % NX ^ across
    plane = planes_of(place[0] // NX ^ 2)[step]
    return plane, [pl.ds(pl.multiple_of(to * HALF + x * 16, 16), 16) for to in range(NX)]


def gather_kernel(place, own, rest, *refs):
    out = refs[-1]
    for part, distance in enumerate((2, 0, 1, 3)):
        out[distance ^ place[1]] = own[part]
    place_rest(place, out, rest, 0)
    for steps, ref in zip(CHUNKS, refs[:-1]):
        for n, (step, across) in enumerate(steps):
            plane, rows = places(place, step, across)
            for to in range(NX):
                out[plane, rows[to], :] += ref[pl.ds(n * HALF + to * 16, 16), :]


def gather(place, own, rest, done):
    vmem = pl.BlockSpec(memory_space=pltpu.VMEM)
    return pl.pallas_call(
        gather_kernel,
        in_specs=[pl.BlockSpec(memory_space=pltpu.SMEM)] + [vmem] * (2 + len(done)),
        out_specs=vmem,
        out_shape=jax.ShapeDtypeStruct((4, PART, WIDTH), jnp.float32),
        compiler_params=params(14),
        cost_estimate=light(),
        name="gather",
    )(place, own, rest, *done)


def finish_kernel(place, sums, rest, last, out, all_sums, total):
    all_sums[...] = sums[...]
    place_rest(place, all_sums, rest, 1)
    value = turn(decoded(last))
    for n, (step, across) in enumerate(CHUNKS[-1]):
        plane, rows = places(place, step, across)
        for to in range(NX):
            start = n * HALF + to * 16
            all_sums[plane, rows[to], :] += value[start : start + 16]
    total[...] = all_sums[...].astype(jnp.bfloat16)
    natural = natural_order()
    value = total[...].reshape(OWNED, WIDTH)
    for p in range(PANELS):
        cut = slice(p * TP, (p + 1) * TP)
        out[:, cut] = matmul(natural, value[:, cut]).astype(jnp.bfloat16)


def finish(place, sums, rest, last):
    vmem = pl.BlockSpec(memory_space=pltpu.VMEM)
    return pl.pallas_call(
        finish_kernel,
        in_specs=[pl.BlockSpec(memory_space=pltpu.SMEM), vmem, vmem, vmem],
        out_specs=vmem,
        out_shape=jax.ShapeDtypeStruct((OWNED, WIDTH), jnp.bfloat16),
        scratch_shapes=[pltpu.VMEM((4, PART, WIDTH), jnp.float32), pltpu.VMEM((4, PART, WIDTH), jnp.bfloat16)],
        compiler_params=params(14),
        cost_estimate=light(),
        name="finish",
    )(place, sums, rest, last)


def coded(value):
    largest = value
    while largest.ndim > 0 and largest.shape != (1,) * value.ndim:
        axis = next(n for n, size in enumerate(largest.shape) if size > 1)
        largest = jnp.max(jnp.abs(largest), axis=axis, keepdims=True)
    power = jnp.ceil(jnp.log2(jnp.maximum(largest, 1e-30)))
    scaled = value * jnp.exp2(7 - power)
    return scaled * jnp.abs(scaled), jnp.broadcast_to(power, (*value.shape[:-1], LANES))


def put_coded(ref, value):
    ref[..., :WIDTH], ref[..., WIDTH:] = coded(value)


def decoded(ref):
    value = ref[..., :WIDTH]
    power = ref[..., WIDTH : WIDTH + 1]
    root = jnp.sqrt(jnp.abs(value)) * jnp.exp2(power - 7)
    return jnp.where(value < 0, -root, root)


def wire(value):
    return value.astype(WIRE)


def unwire(value):
    return value.astype(jnp.float32)


def small_kernel(kernel, shapes, mib, name):
    vmem = pl.BlockSpec(memory_space=pltpu.VMEM)
    shapes = [jax.ShapeDtypeStruct(shape, jnp.float32) for shape in shapes]
    return pl.pallas_call(
        kernel,
        out_specs=[vmem] * len(shapes),
        out_shape=shapes,
        compiler_params=params(mib),
        cost_estimate=light(),
        name=name,
    )


def add_cores_kernel(part, sibling, pair, out):
    for n in (0, 1, 2, 3):
        pair[n] = part[n] + sibling[3 - n]
    put_coded(out, pair[0])


def add_cores(part):
    call = small_kernel(add_cores_kernel, [part.shape, (part.shape[1], WIDTH + LANES)], 12, "add_cores")
    return call(part, across_core(part))


def add_chips_kernel(pair, over, mine, out):
    mine[...] = pair[1] + decoded(over)
    put_coded(out, mine[...])


def add_chips(pair, over):
    call = small_kernel(add_chips_kernel, [pair.shape[1:], over.shape], 8, "add_chips")
    return call(pair, unwire(over))


def together(*values):
    return lax.optimization_barrier(values)


def on_device(amplitudes, integrals, tile_irrep, product_pairs, summed_pairs):
    row, col = lax.axis_index("row"), lax.axis_index("col")
    z = row // NX
    place = jnp.stack([row, col]).astype(jnp.int32)
    tables = (place, tile_irrep, product_pairs, summed_pairs)
    inner = (z == 1) | (z == 2)
    outward = {0: 1, 1: 0, 2: 3, 3: 2}
    inward = {1: 2, 2: 1}

    here0 = amplitudes
    beside0 = across_x(here0)
    here1 = along_z(here0, outward)
    middle = along_z(here0, inward)
    part0 = partial_ladder(tables, integrals, here0)
    beside0, here1, middle, part0 = together(beside0, here1, middle, part0)

    beside1 = across_x(here1)
    crossed = along_z(here1, inward)
    here2 = along_z(middle, outward)
    pair0, sent = add_cores(part0)
    over0 = across_y(wire(sent))
    part1 = partial_ladder(tables, integrals, beside0, here1)
    beside1, crossed, here2, pair0, over0, part1 = together(beside1, crossed, here2, pair0, over0, part1)
    here2 = jnp.where(inner, middle, here2)

    beside2 = across_x(here2)
    here3 = along_z(crossed, outward)
    mine0, sent = add_chips(pair0, over0)
    other0 = to_partner(wire(sent))
    pair1, sent = add_cores(part1)
    over1 = across_y(wire(sent))
    part2 = partial_ladder(tables, integrals, beside1, here2)
    own = sort_own(place, CHUNKS[0], pair0, mine0)
    owed_here = sort_owed(place, 0, pair0)
    beside2, here3, other0, own, owed_here, pair1, over1, part2 = together(
        beside2, here3, other0, own, owed_here, pair1, over1, part2
    )
    here3 = jnp.where(inner, crossed, here3)

    beside3 = across_x(here3)
    mine1, sent = add_chips(pair1, over1)
    other1 = to_partner(wire(sent))
    pair2, sent = add_cores(part2)
    over2 = across_y(wire(sent))
    part3 = partial_ladder(tables, integrals, beside2, here3)
    own = sort_own(place, CHUNKS[1], pair1, mine1, own)
    owed_beside = sort_owed(place, 0, pair1, across=1)
    owed_here = sort_owed(place, 1, pair1, owed_here)
    beside3, other0, other1, own, owed_here, owed_beside, pair2, over2, part3 = together(
        beside3, other0, other1, own, owed_here, owed_beside, pair2, over2, part3
    )

    mine2, sent = add_chips(pair2, over2)
    other2 = to_partner(wire(sent))
    pair3, sent = add_cores(part3)
    over3 = across_y(wire(sent))
    part4 = partial_ladder(tables, integrals, beside3)
    own = sort_own(place, CHUNKS[2], pair2, mine2, own)
    owed_beside = sort_owed(place, 1, pair2, owed_beside, across=1)
    owed_here = sort_owed(place, 2, pair2, owed_here)
    owed_beside = sort_owed(place, 2, pair3, owed_beside, across=1)
    owed_here = wire(sort_owed(place, 3, pair3, owed_here))
    other0, other1, other2, own, owed_here, owed_beside, pair3, over3, part4 = together(
        other0, other1, other2, own, owed_here, owed_beside, pair3, over3, part4
    )

    mine3, sent = add_chips(pair3, over3)
    sent, owed_here = together(wire(sent), owed_here)
    other3 = to_partner(sent)
    came_here = across_y(owed_here)
    pair4, sent = add_cores(part4)
    over4 = across_y(wire(sent))
    own = sort_own(place, CHUNKS[3], pair3, mine3, own)
    owed_beside = wire(sort_owed(place, 3, pair4, owed_beside, across=1))
    other0, other1, other2, other3, own, came_here, pair4, over4 = together(
        other0, other1, other2, other3, own, came_here, pair4, over4
    )

    mine4, sent = add_chips(pair4, over4)
    sent, *others = together(sent, other0, other1, other2, other3)
    other4 = to_partner(wire(sent))
    came_beside = across_y(owed_beside)
    own = sort_own(place, CHUNKS[4], pair4, mine4, own)
    done = [turned(unwire(other)) for other in others]
    sums = gather(place, own, unwire(came_here), done)
    return finish(place, sums, unwire(came_beside), unwire(other4))


def solution(mesh):
    body = on_device if (mesh.shape["row"], mesh.shape["col"]) == (NZ * NX, NY * NC) else plain
    return jax.shard_map(
        body,
        mesh=mesh,
        in_specs=(P("row", "col"), P("col", "row"), P(), P("row", None), P("col", None)),
        out_specs=P("col", "row"),
        check_vma=False,
    )
```

```python
import functools

import jax
import jax.numpy as jnp
import numpy as np
from jax import lax
from jax.experimental import pallas as pl
from jax.experimental.pallas import tpu as pltpu
from jax.sharding import PartitionSpec as P

TS = 16
TP = TS * TS
OT = 32
WIRE = jnp.float16


def from_partner(value, axis, distance):
    mask = 2**distance
    pairs = [(source, source ^ mask) for source in range(lax.axis_size(axis))]
    return lax.ppermute(value, axis, pairs)


def pair_symmetry(tile_irrep, pairs):
    return jnp.bitwise_xor(tile_irrep[pairs[:, 0]], tile_irrep[pairs[:, 1]])


def plain(amplitudes, integrals, tile_irrep, product_pairs, summed_pairs):
    product_sym = pair_symmetry(tile_irrep, product_pairs)
    summed_sym = pair_symmetry(tile_irrep, summed_pairs)
    allowed = summed_sym[:, None] == product_sym[None, :]
    summed_count = summed_pairs.shape[0]
    product_count = product_pairs.shape[0]
    keep = allowed.astype(integrals.dtype)
    masked = (
        integrals.reshape(summed_count, TP, product_count, TP)
        * keep[:, None, :, None]
    ).reshape(integrals.shape)
    half_bit = lax.axis_size("row").bit_length() - 2
    ladder = jnp.dot(
        lax.all_gather(amplitudes, "row", axis=0, tiled=True),
        masked,
        preferred_element_type=jnp.float32,
    )
    partner = from_partner(ladder, "row", half_bit)
    partner = partner.reshape(OT, OT, product_count, TS, TS)
    partner = jnp.transpose(partner, (1, 0, 2, 4, 3)).reshape(ladder.shape)
    summed = lax.psum_scatter(ladder + partner, "col", scatter_dimension=0, tiled=True)
    return summed.astype(jnp.bfloat16)


NZ, NX, NY, NC = 4, 2, 2, 2
ROWS = 128
HALF = 32
PART = 2 * HALF
OWNED = 256
WIDTH = 2048
PANELS = WIDTH // TP
LANES = 128
EXTRA = 16
PLANES = ((0, 1, 2, 3), (1, 0, 2, 3), (2, 3, 1, 0), (3, 2, 1, 0))
PART_OF = (1, 2, 0, 3)


CHUNKS = (((0, 0),), ((0, 1), (1, 0)), ((1, 1), (2, 0)), ((2, 1), (3, 0)), ((3, 1),))


def params(mib):
    return pltpu.CompilerParams(vmem_limit_bytes=mib * 2**20)


def light():
    return pl.CostEstimate(flops=1000, bytes_accessed=1000, transcendentals=0)


def selection(extents, axes):
    n = int(np.prod(extents))
    row = lax.broadcasted_iota(jnp.int32, (n, n), 0)
    column = lax.broadcasted_iota(jnp.int32, (n, n), 1)
    strides = [int(np.prod(extents[axis + 1 :])) for axis in range(len(extents))]
    source, below = jnp.zeros_like(row), 1
    for axis in reversed(axes):
        source += row // below % extents[axis] * strides[axis]
        below *= extents[axis]
    return jnp.where(source == column, 1.0, 0.0).astype(jnp.bfloat16)


def block_order():
    return selection((4, 32), (1, 0))


def align_order():
    return selection((2, 4, 4), (0, 2, 1))


def natural_order():
    return selection((4, 2, 8, 4), (1, 3, 0, 2))


def swap_order():
    return selection((TS, TS), (1, 0))


def send(value, target):
    pairs = []
    for n, (z, x, y, k) in enumerate(np.ndindex(NZ, NX, NY, NC)):
        to = target(z, x, y, k)
        if to is not None:
            pairs.append((n, int(np.ravel_multi_index(to, (NZ, NX, NY, NC)))))
    return lax.ppermute(value, ("row", "col"), pairs)


def along_z(value, moves):
    return send(value, lambda z, x, y, k: (moves[z], x, y, k) if z in moves else None)


def across_x(value, planes=range(NZ)):
    return send(value, lambda z, x, y, k: (z, 1 - x, y, k) if z in planes else None)


def across_y(value):
    return send(value, lambda z, x, y, k: (z, x, 1 - y, k))


def across_core(value):
    return send(value, lambda z, x, y, k: (z, x, y, 1 - k))


def to_partner(value):
    return send(value, lambda z, x, y, k: (z ^ 2, x, y, k))


def matmul(a, b):
    return jnp.dot(a, b, preferred_element_type=jnp.float32)


def lookup(table, index):
    value = table[0]
    for n in range(1, len(table)):
        value = jnp.where(index == n, table[n], value)
    return value


def ladder_kernel(place, irrep, product, summed, *refs):
    blocks, (integrals, out, rows) = refs[:-3], refs[-3:]
    order = block_order()
    for n, block in enumerate(blocks):
        rows[n * ROWS : (n + 1) * ROWS, :] = matmul(order, block[...]).astype(jnp.bfloat16)
    for p in range(PANELS):
        wanted = irrep[product[p, 0]] ^ irrep[product[p, 1]]
        kept = []
        for q in range(WIDTH // TP):
            same = (irrep[summed[q, 0]] ^ irrep[summed[q, 1]]) == wanted
            value = rows[:, q * TP : (q + 1) * TP]
            kept.append(jnp.where(same, value, jnp.zeros_like(value)))
        cut = slice(p * TP, (p + 1) * TP)
        total = matmul(jnp.concatenate(kept, axis=1), integrals[:, cut])
        for to in range(4):
            for n in range(len(blocks)):
                start = n * ROWS + to * HALF
                out[lookup(PART_OF, to ^ place[1]), n * HALF : (n + 1) * HALF, cut] = total[start : start + HALF, :]


def partial_ladder(tables, integrals, *blocks):
    vmem = pl.BlockSpec(memory_space=pltpu.VMEM)
    return pl.pallas_call(
        ladder_kernel,
        in_specs=[pl.BlockSpec(memory_space=pltpu.SMEM)] * 4 + [vmem] * (len(blocks) + 1),
        out_specs=vmem,
        scratch_shapes=[pltpu.VMEM((len(blocks) * ROWS, WIDTH), jnp.bfloat16)],
        out_shape=jax.ShapeDtypeStruct((4, len(blocks) * HALF, WIDTH), jnp.float32),
        compiler_params=params(14),
        cost_estimate=light(),
        name="partial_ladder",
    )(*tables, *blocks, integrals)


def turn(arrived):
    high = arrived.astype(jnp.bfloat16)
    low = (arrived - high.astype(jnp.float32)).astype(jnp.bfloat16)
    both = jnp.concatenate([high, low], axis=0)
    swap, align = swap_order(), align_order()
    cuts = [both[:, p * TP : (p + 1) * TP] for p in range(PANELS)]
    both = jnp.concatenate([matmul(cut, swap).astype(jnp.bfloat16) for cut in cuts], axis=1)
    halves = [matmul(align, both[n : n + HALF]) for n in range(0, both.shape[0], HALF)]
    count = len(halves) // 2
    return jnp.concatenate([high + low for high, low in zip(halves[:count], halves[count:], strict=True)], axis=0)


def turn_kernel(arrived, out):
    out[...] = turn(decoded(arrived))


def turned(arrived):
    return pl.pallas_call(
        turn_kernel,
        out_shape=jax.ShapeDtypeStruct(((arrived.shape[0] - EXTRA) * LANES // WIDTH, WIDTH), jnp.float32),
        compiler_params=params(12),
        cost_estimate=pl.CostEstimate(flops=8 * 10**8, bytes_accessed=10**6, transcendentals=0),
        name="turn",
    )(arrived)


def planes_of(side):
    return [lookup([planes[step] for planes in PLANES], side) for step in range(4)]


def sort_own_kernel(steps, place, pair, mine, *refs):
    own, sems = refs[-2:]
    for n, (step, across) in enumerate(steps):

        @pl.when(planes_of(place[0] // NX)[step] == place[1])
        def _(n=n, across=across):
            rows = pl.ds(n * HALF, HALF)
            to = pl.ds(pl.multiple_of((place[0] % NX ^ across) * HALF, HALF), HALF)
            copies = [
                pltpu.make_async_copy(pair.at[0, rows], own.at[0, to], sems.at[0]),
                pltpu.make_async_copy(mine.at[rows], own.at[1, to], sems.at[1]),
                pltpu.make_async_copy(pair.at[pl.ds(2, 2), rows], own.at[pl.ds(2, 2), to], sems.at[2]),
            ]
            for copy in copies:
                copy.start()
            for copy in copies:
                copy.wait()


def sort_owed_kernel(steps, place, pair, *refs):
    owed, buffer, sem = refs[-3:]
    ((n, step),) = steps

    @pl.when(planes_of(place[0] // NX)[step] == place[1] ^ 2)
    def _():
        put_coded(buffer, pair[1:, n * HALF : (n + 1) * HALF])
        copy = pltpu.make_async_copy(buffer, owed, sem)
        copy.start()
        copy.wait()


def sort(kernel, shape, scratch, place, steps, values, before):
    vmem = pl.BlockSpec(memory_space=pltpu.VMEM)
    hbm = pl.BlockSpec(memory_space=pl.ANY)
    before = [] if before is None else [before]
    return pl.pallas_call(
        functools.partial(kernel, steps),
        in_specs=[pl.BlockSpec(memory_space=pltpu.SMEM)] + [vmem] * len(values) + [hbm] * len(before),
        out_specs=hbm,
        out_shape=jax.ShapeDtypeStruct(shape, jnp.float32),
        scratch_shapes=scratch,
        input_output_aliases={1 + len(values): 0} if before else {},
        compiler_params=params(10),
        cost_estimate=light(),
        name="sort",
    )(place, *values, *before)


def sort_own(place, steps, pair, mine, before=None):
    return sort(sort_own_kernel, (4, PART, WIDTH), [pltpu.SemaphoreType.DMA((3,))], place, steps, (pair, mine), before)


def sort_owed(place, step, pair, before=None, across=0):
    n = next(n for chunk in CHUNKS for n, block in enumerate(chunk) if block == (step, across))
    scratch = [pltpu.VMEM((3, wire_rows(HALF), LANES), jnp.float32), pltpu.SemaphoreType.DMA]
    return sort(sort_owed_kernel, (3, wire_rows(HALF), LANES), scratch, place, ((n, step),), (pair,), before)


def place_rest(place, ref, rest, across):
    rows = pl.ds(pl.multiple_of((place[0] % NX ^ across) * HALF, HALF), HALF)
    for came, distance in enumerate((0, 1, 3)):
        ref[distance ^ 2 ^ place[1], rows, :] += decoded(rest.at[came])


def places(place, step, across):
    x = place[0] % NX ^ across
    plane = planes_of(place[0] // NX ^ 2)[step]
    return plane, [pl.ds(pl.multiple_of(to * HALF + x * 16, 16), 16) for to in range(NX)]


def gather_kernel(place, own, rest, *refs):
    out = refs[-1]
    for part, distance in enumerate((2, 0, 1, 3)):
        out[distance ^ place[1]] = own[part]
    place_rest(place, out, rest, 0)
    for steps, ref in zip(CHUNKS, refs[:-1]):
        for n, (step, across) in enumerate(steps):
            plane, rows = places(place, step, across)
            for to in range(NX):
                out[plane, rows[to], :] += ref[pl.ds(n * HALF + to * 16, 16), :]


def gather(place, own, rest, done):
    vmem = pl.BlockSpec(memory_space=pltpu.VMEM)
    return pl.pallas_call(
        gather_kernel,
        in_specs=[pl.BlockSpec(memory_space=pltpu.SMEM)] + [vmem] * (2 + len(done)),
        out_specs=vmem,
        out_shape=jax.ShapeDtypeStruct((4, PART, WIDTH), jnp.float32),
        compiler_params=params(14),
        cost_estimate=light(),
        name="gather",
    )(place, own, rest, *done)


def finish_kernel(place, sums, rest, last, out, all_sums, total):
    all_sums[...] = sums[...]
    place_rest(place, all_sums, rest, 1)
    value = turn(decoded(last))
    for n, (step, across) in enumerate(CHUNKS[-1]):
        plane, rows = places(place, step, across)
        for to in range(NX):
            start = n * HALF + to * 16
            all_sums[plane, rows[to], :] += value[start : start + 16]
    total[...] = all_sums[...].astype(jnp.bfloat16)
    natural = natural_order()
    value = total[...].reshape(OWNED, WIDTH)
    for p in range(PANELS):
        cut = slice(p * TP, (p + 1) * TP)
        out[:, cut] = matmul(natural, value[:, cut]).astype(jnp.bfloat16)


def finish(place, sums, rest, last):
    vmem = pl.BlockSpec(memory_space=pltpu.VMEM)
    return pl.pallas_call(
        finish_kernel,
        in_specs=[pl.BlockSpec(memory_space=pltpu.SMEM), vmem, vmem, vmem],
        out_specs=vmem,
        out_shape=jax.ShapeDtypeStruct((OWNED, WIDTH), jnp.bfloat16),
        scratch_shapes=[pltpu.VMEM((4, PART, WIDTH), jnp.float32), pltpu.VMEM((4, PART, WIDTH), jnp.bfloat16)],
        compiler_params=params(14),
        cost_estimate=light(),
        name="finish",
    )(place, sums, rest, last)


def wire_rows(rows):
    return rows * (WIDTH // LANES) + EXTRA


def put_coded(ref, value):
    largest = value
    while largest.shape != (1,) * value.ndim:
        axis = next(n for n, size in enumerate(largest.shape) if size > 1)
        largest = jnp.max(jnp.abs(largest), axis=axis, keepdims=True)
    power = jnp.ceil(jnp.log2(jnp.maximum(largest, 1e-30)))
    scaled = value * jnp.exp2(7 - power)
    scaled = scaled * jnp.abs(scaled)
    rows = value.shape[-2]
    for n in range(WIDTH // LANES):
        ref[..., n * rows : (n + 1) * rows, :] = scaled[..., n * LANES : (n + 1) * LANES]
    ref[..., ref.shape[-2] - EXTRA :, :] = jnp.broadcast_to(power, (*value.shape[:-2], EXTRA, LANES))


def decoded(ref):
    rows = (ref.shape[0] - EXTRA) * LANES // WIDTH
    value = jnp.concatenate([ref[n * rows : (n + 1) * rows, :] for n in range(WIDTH // LANES)], axis=1)
    power = ref[ref.shape[0] - EXTRA : ref.shape[0] - EXTRA + 1, 0:1]
    root = jnp.sqrt(jnp.abs(value)) * jnp.exp2(power - 7)
    return jnp.where(value < 0, -root, root)


def wire(value):
    return value.astype(WIRE)


def unwire(value):
    return value.astype(jnp.float32)


def small_kernel(kernel, shapes, mib, name):
    vmem = pl.BlockSpec(memory_space=pltpu.VMEM)
    shapes = [jax.ShapeDtypeStruct(shape, jnp.float32) for shape in shapes]
    return pl.pallas_call(
        kernel,
        out_specs=[vmem] * len(shapes),
        out_shape=shapes,
        compiler_params=params(mib),
        cost_estimate=light(),
        name=name,
    )


def add_cores_kernel(part, sibling, pair, out):
    for n in (0, 1, 2, 3):
        pair[n] = part[n] + sibling[3 - n]
    put_coded(out, pair[0])


def add_cores(part):
    call = small_kernel(add_cores_kernel, [part.shape, (wire_rows(part.shape[1]), LANES)], 12, "add_cores")
    return call(part, across_core(part))


def add_chips_kernel(pair, over, mine, out):
    mine[...] = pair[1] + decoded(over)
    put_coded(out, mine[...])


def add_chips(pair, over):
    call = small_kernel(add_chips_kernel, [pair.shape[1:], over.shape], 8, "add_chips")
    return call(pair, unwire(over))


def together(*values):
    return lax.optimization_barrier(values)


def on_device(amplitudes, integrals, tile_irrep, product_pairs, summed_pairs):
    row, col = lax.axis_index("row"), lax.axis_index("col")
    z = row // NX
    place = jnp.stack([row, col]).astype(jnp.int32)
    tables = (place, tile_irrep, product_pairs, summed_pairs)
    inner = (z == 1) | (z == 2)
    outward = {0: 1, 1: 0, 2: 3, 3: 2}
    inward = {1: 2, 2: 1}

    here0 = amplitudes
    beside0 = across_x(here0)
    here1 = along_z(here0, outward)
    middle = along_z(here0, inward)
    part0 = partial_ladder(tables, integrals, here0)
    beside0, here1, middle, part0 = together(beside0, here1, middle, part0)

    beside1 = across_x(here1)
    crossed = along_z(here1, inward)
    here2 = along_z(middle, outward)
    pair0, sent = add_cores(part0)
    over0 = across_y(wire(sent))
    part1 = partial_ladder(tables, integrals, beside0, here1)
    here2 = jnp.where(inner, middle, here2)
    beside1, crossed, here2, pair0, over0, part1 = together(beside1, crossed, here2, pair0, over0, part1)

    beside2 = across_x(here2)
    here3 = along_z(crossed, outward)
    mine0, sent = add_chips(pair0, over0)
    other0 = to_partner(wire(sent))
    pair1, sent = add_cores(part1)
    over1 = across_y(wire(sent))
    part2 = partial_ladder(tables, integrals, beside1, here2)
    own = sort_own(place, CHUNKS[0], pair0, mine0)
    owed_here = sort_owed(place, 0, pair0)
    beside2, here3, other0, own, owed_here, pair1, over1, part2 = together(
        beside2, here3, other0, own, owed_here, pair1, over1, part2
    )
    here3 = jnp.where(inner, crossed, here3)

    beside3 = across_x(here3)
    mine1, sent = add_chips(pair1, over1)
    other1 = to_partner(wire(sent))
    pair2, sent = add_cores(part2)
    over2 = across_y(wire(sent))
    part3 = partial_ladder(tables, integrals, beside2, here3)
    own = sort_own(place, CHUNKS[1], pair1, mine1, own)
    owed_beside = sort_owed(place, 0, pair1, across=1)
    owed_here = sort_owed(place, 1, pair1, owed_here)
    beside3, other0, other1, own, owed_here, owed_beside, pair2, over2, part3 = together(
        beside3, other0, other1, own, owed_here, owed_beside, pair2, over2, part3
    )

    mine2, sent = add_chips(pair2, over2)
    other2 = to_partner(wire(sent))
    pair3, sent = add_cores(part3)
    over3 = across_y(wire(sent))
    part4 = partial_ladder(tables, integrals, beside3)
    own = sort_own(place, CHUNKS[2], pair2, mine2, own)
    owed_beside = sort_owed(place, 1, pair2, owed_beside, across=1)
    owed_here = sort_owed(place, 2, pair2, owed_here)
    owed_beside = sort_owed(place, 2, pair3, owed_beside, across=1)
    owed_here = wire(sort_owed(place, 3, pair3, owed_here))
    other0, other1, other2, own, owed_here, owed_beside, pair3, over3, part4 = together(
        other0, other1, other2, own, owed_here, owed_beside, pair3, over3, part4
    )

    mine3, sent = add_chips(pair3, over3)
    sent, owed_here = together(wire(sent), owed_here)
    other3 = to_partner(sent)
    came_here = across_y(owed_here)
    pair4, sent = add_cores(part4)
    over4 = across_y(wire(sent))
    own = sort_own(place, CHUNKS[3], pair3, mine3, own)
    owed_beside = wire(sort_owed(place, 3, pair4, owed_beside, across=1))
    mine4, ready4 = add_chips(pair4, over4)
    other0, other1, other2, other3, own, came_here, pair4, mine4, ready4 = together(
        other0, other1, other2, other3, own, came_here, pair4, mine4, ready4
    )

    sent, *others = together(ready4, other0, other1, other2, other3)
    other4 = to_partner(wire(sent))
    came_beside = across_y(owed_beside)
    own = sort_own(place, CHUNKS[4], pair4, mine4, own)
    done = [turned(unwire(other)) for other in others]
    sums = gather(place, own, unwire(came_here), done)
    return finish(place, sums, unwire(came_beside), unwire(other4))


def solution(mesh):
    body = on_device if (mesh.shape["row"], mesh.shape["col"]) == (NZ * NX, NY * NC) else plain
    return jax.shard_map(
        body,
        mesh=mesh,
        in_specs=(P("row", "col"), P("col", "row"), P(), P("row", None), P("col", None)),
        out_specs=P("col", "row"),
        check_vma=False,
    )
```

```python
import functools

import jax
import jax.numpy as jnp
import numpy as np
from jax import lax
from jax.experimental import pallas as pl
from jax.experimental.pallas import tpu as pltpu
from jax.sharding import PartitionSpec as P

TS = 16
TP = TS * TS
OT = 32
WIRE = jnp.float16


def from_partner(value, axis, distance):
    mask = 2**distance
    pairs = [(source, source ^ mask) for source in range(lax.axis_size(axis))]
    return lax.ppermute(value, axis, pairs)


def pair_symmetry(tile_irrep, pairs):
    return jnp.bitwise_xor(tile_irrep[pairs[:, 0]], tile_irrep[pairs[:, 1]])


def plain(amplitudes, integrals, tile_irrep, product_pairs, summed_pairs):
    product_sym = pair_symmetry(tile_irrep, product_pairs)
    summed_sym = pair_symmetry(tile_irrep, summed_pairs)
    allowed = summed_sym[:, None] == product_sym[None, :]
    summed_count = summed_pairs.shape[0]
    product_count = product_pairs.shape[0]
    keep = allowed.astype(integrals.dtype)
    masked = (
        integrals.reshape(summed_count, TP, product_count, TP)
        * keep[:, None, :, None]
    ).reshape(integrals.shape)
    half_bit = lax.axis_size("row").bit_length() - 2
    ladder = jnp.dot(
        lax.all_gather(amplitudes, "row", axis=0, tiled=True),
        masked,
        preferred_element_type=jnp.float32,
    )
    partner = from_partner(ladder, "row", half_bit)
    partner = partner.reshape(OT, OT, product_count, TS, TS)
    partner = jnp.transpose(partner, (1, 0, 2, 4, 3)).reshape(ladder.shape)
    summed = lax.psum_scatter(ladder + partner, "col", scatter_dimension=0, tiled=True)
    return summed.astype(jnp.bfloat16)


NZ, NX, NY, NC = 4, 2, 2, 2
ROWS = 128
HALF = 32
PART = 2 * HALF
OWNED = 256
WIDTH = 2048
PANELS = WIDTH // TP
LANES = 128
EXTRA = 16
PLANES = ((0, 1, 2, 3), (1, 0, 2, 3), (2, 3, 1, 0), (3, 2, 1, 0))
PART_OF = (1, 2, 0, 3)


CHUNKS = (((0, 0),), ((0, 1), (1, 0)), ((1, 1), (2, 0)), ((2, 1), (3, 0)), ((3, 1),))


def params(mib):
    return pltpu.CompilerParams(vmem_limit_bytes=mib * 2**20)


def light():
    return pl.CostEstimate(flops=1000, bytes_accessed=1000, transcendentals=0)


def selection(extents, axes):
    n = int(np.prod(extents))
    row = lax.broadcasted_iota(jnp.int32, (n, n), 0)
    column = lax.broadcasted_iota(jnp.int32, (n, n), 1)
    strides = [int(np.prod(extents[axis + 1 :])) for axis in range(len(extents))]
    source, below = jnp.zeros_like(row), 1
    for axis in reversed(axes):
        source += row // below % extents[axis] * strides[axis]
        below *= extents[axis]
    return jnp.where(source == column, 1.0, 0.0).astype(jnp.bfloat16)


def block_order():
    return selection((4, 32), (1, 0))


def align_order():
    return selection((2, 4, 4), (0, 2, 1))


def natural_order():
    return selection((4, 2, 8, 4), (1, 3, 0, 2))


def swap_order():
    return selection((TS, TS), (1, 0))


def send(value, target):
    pairs = []
    for n, (z, x, y, k) in enumerate(np.ndindex(NZ, NX, NY, NC)):
        to = target(z, x, y, k)
        if to is not None:
            pairs.append((n, int(np.ravel_multi_index(to, (NZ, NX, NY, NC)))))
    return lax.ppermute(value, ("row", "col"), pairs)


def along_z(value, moves):
    return send(value, lambda z, x, y, k: (moves[z], x, y, k) if z in moves else None)


def across_x(value, planes=range(NZ)):
    return send(value, lambda z, x, y, k: (z, 1 - x, y, k) if z in planes else None)


def across_y(value):
    return send(value, lambda z, x, y, k: (z, x, 1 - y, k))


def across_core(value):
    return send(value, lambda z, x, y, k: (z, x, y, 1 - k))


def to_partner(value):
    return send(value, lambda z, x, y, k: (z ^ 2, x, y, k))


def matmul(a, b):
    return jnp.dot(a, b, preferred_element_type=jnp.float32)


def lookup(table, index):
    value = table[0]
    for n in range(1, len(table)):
        value = jnp.where(index == n, table[n], value)
    return value


def ladder_kernel(place, irrep, product, summed, *refs):
    blocks, (integrals, out, rows) = refs[:-3], refs[-3:]
    order = block_order()
    for n, block in enumerate(blocks):
        rows[n * ROWS : (n + 1) * ROWS, :] = matmul(order, block[...]).astype(jnp.bfloat16)
    for p in range(PANELS):
        wanted = irrep[product[p, 0]] ^ irrep[product[p, 1]]
        kept = []
        for q in range(WIDTH // TP):
            same = (irrep[summed[q, 0]] ^ irrep[summed[q, 1]]) == wanted
            value = rows[:, q * TP : (q + 1) * TP]
            kept.append(jnp.where(same, value, jnp.zeros_like(value)))
        cut = slice(p * TP, (p + 1) * TP)
        total = matmul(jnp.concatenate(kept, axis=1), integrals[:, cut])
        for to in range(4):
            for n in range(len(blocks)):
                start = n * ROWS + to * HALF
                out[lookup(PART_OF, to ^ place[1]), n * HALF : (n + 1) * HALF, cut] = total[start : start + HALF, :]


def partial_ladder(tables, integrals, *blocks):
    vmem = pl.BlockSpec(memory_space=pltpu.VMEM)
    return pl.pallas_call(
        ladder_kernel,
        in_specs=[pl.BlockSpec(memory_space=pltpu.SMEM)] * 4 + [vmem] * (len(blocks) + 1),
        out_specs=vmem,
        scratch_shapes=[pltpu.VMEM((len(blocks) * ROWS, WIDTH), jnp.bfloat16)],
        out_shape=jax.ShapeDtypeStruct((4, len(blocks) * HALF, WIDTH), jnp.float32),
        compiler_params=params(14),
        cost_estimate=light(),
        name="partial_ladder",
    )(*tables, *blocks, integrals)


def turn(arrived):
    high = arrived.astype(jnp.bfloat16)
    low = (arrived - high.astype(jnp.float32)).astype(jnp.bfloat16)
    both = jnp.concatenate([high, low], axis=0)
    swap, align = swap_order(), align_order()
    cuts = [both[:, p * TP : (p + 1) * TP] for p in range(PANELS)]
    both = jnp.concatenate([matmul(cut, swap).astype(jnp.bfloat16) for cut in cuts], axis=1)
    halves = [matmul(align, both[n : n + HALF]) for n in range(0, both.shape[0], HALF)]
    count = len(halves) // 2
    return jnp.concatenate([high + low for high, low in zip(halves[:count], halves[count:], strict=True)], axis=0)


def turn_kernel(arrived, out):
    out[...] = turn(decoded(arrived))


def turned(arrived):
    return pl.pallas_call(
        turn_kernel,
        out_shape=jax.ShapeDtypeStruct(((arrived.shape[0] - EXTRA) * LANES // WIDTH, WIDTH), jnp.float32),
        compiler_params=params(12),
        cost_estimate=pl.CostEstimate(flops=8 * 10**8, bytes_accessed=10**6, transcendentals=0),
        name="turn",
    )(arrived)


def planes_of(side):
    return [lookup([planes[step] for planes in PLANES], side) for step in range(4)]


def sort_own_kernel(steps, place, pair, mine, *refs):
    own, sems = refs[-2:]
    for n, (step, across) in enumerate(steps):

        @pl.when(planes_of(place[0] // NX)[step] == place[1])
        def _(n=n, across=across):
            rows = pl.ds(n * HALF, HALF)
            to = pl.ds(pl.multiple_of((place[0] % NX ^ across) * HALF, HALF), HALF)
            copies = [
                pltpu.make_async_copy(pair.at[0, rows], own.at[0, to], sems.at[0]),
                pltpu.make_async_copy(mine.at[rows], own.at[1, to], sems.at[1]),
                pltpu.make_async_copy(pair.at[pl.ds(2, 2), rows], own.at[pl.ds(2, 2), to], sems.at[2]),
            ]
            for copy in copies:
                copy.start()
            for copy in copies:
                copy.wait()


def sort_owed_kernel(steps, place, pair, *refs):
    owed, buffer, sem = refs[-3:]
    ((n, step),) = steps

    @pl.when(planes_of(place[0] // NX)[step] == place[1] ^ 2)
    def _():
        put_coded(buffer, pair[1:, n * HALF : (n + 1) * HALF])
        copy = pltpu.make_async_copy(buffer, owed, sem)
        copy.start()
        copy.wait()


def sort(kernel, shape, scratch, place, steps, values, before):
    vmem = pl.BlockSpec(memory_space=pltpu.VMEM)
    hbm = pl.BlockSpec(memory_space=pl.ANY)
    before = [] if before is None else [before]
    return pl.pallas_call(
        functools.partial(kernel, steps),
        in_specs=[pl.BlockSpec(memory_space=pltpu.SMEM)] + [vmem] * len(values) + [hbm] * len(before),
        out_specs=hbm,
        out_shape=jax.ShapeDtypeStruct(shape, jnp.float32),
        scratch_shapes=scratch,
        input_output_aliases={1 + len(values): 0} if before else {},
        compiler_params=params(10),
        cost_estimate=light(),
        name="sort",
    )(place, *values, *before)


def sort_own(place, steps, pair, mine, before=None):
    return sort(sort_own_kernel, (4, PART, WIDTH), [pltpu.SemaphoreType.DMA((3,))], place, steps, (pair, mine), before)


def sort_owed(place, step, pair, before=None, across=0):
    n = next(n for chunk in CHUNKS for n, block in enumerate(chunk) if block == (step, across))
    scratch = [pltpu.VMEM((3, wire_rows(HALF), LANES), jnp.float32), pltpu.SemaphoreType.DMA]
    return sort(sort_owed_kernel, (3, wire_rows(HALF), LANES), scratch, place, ((n, step),), (pair,), before)


def place_rest(place, ref, rest, across):
    rows = pl.ds(pl.multiple_of((place[0] % NX ^ across) * HALF, HALF), HALF)
    for came, distance in enumerate((0, 1, 3)):
        ref[distance ^ 2 ^ place[1], rows, :] += decoded(rest.at[came])


def places(place, step, across):
    x = place[0] % NX ^ across
    plane = planes_of(place[0] // NX ^ 2)[step]
    return plane, [pl.ds(pl.multiple_of(to * HALF + x * 16, 16), 16) for to in range(NX)]


def gather_kernel(place, own, rest, *refs):
    out = refs[-1]
    for part, distance in enumerate((2, 0, 1, 3)):
        out[distance ^ place[1]] = own[part]
    place_rest(place, out, rest, 0)
    for steps, ref in zip(CHUNKS, refs[:-1]):
        for n, (step, across) in enumerate(steps):
            plane, rows = places(place, step, across)
            for to in range(NX):
                out[plane, rows[to], :] += ref[pl.ds(n * HALF + to * 16, 16), :]


def gather(place, own, rest, done):
    vmem = pl.BlockSpec(memory_space=pltpu.VMEM)
    return pl.pallas_call(
        gather_kernel,
        in_specs=[pl.BlockSpec(memory_space=pltpu.SMEM)] + [vmem] * (2 + len(done)),
        out_specs=vmem,
        out_shape=jax.ShapeDtypeStruct((4, PART, WIDTH), jnp.float32),
        compiler_params=params(14),
        cost_estimate=light(),
        name="gather",
    )(place, own, rest, *done)


def finish_kernel(place, sums, rest, last, out, all_sums, total, result, sems):
    all_sums[...] = sums[...]
    place_rest(place, all_sums, rest, 1)
    value = turn(decoded(last))
    for n, (step, across) in enumerate(CHUNKS[-1]):
        plane, rows = places(place, step, across)
        for to in range(NX):
            start = n * HALF + to * 16
            all_sums[plane, rows[to], :] += value[start : start + 16]
    total[...] = all_sums[...].astype(jnp.bfloat16)
    natural = natural_order()
    value = total[...].reshape(OWNED, WIDTH)
    copies = []
    for p in range(PANELS):
        cut = slice(p * TP, (p + 1) * TP)
        result[:, cut] = matmul(natural, value[:, cut]).astype(jnp.bfloat16)
        copies.append(pltpu.make_async_copy(result.at[:, pl.ds(p * TP, TP)], out.at[:, pl.ds(p * TP, TP)], sems.at[p]))
        copies[-1].start()
    for copy in copies:
        copy.wait()


def finish(place, sums, rest, last):
    vmem = pl.BlockSpec(memory_space=pltpu.VMEM)
    return pl.pallas_call(
        finish_kernel,
        in_specs=[pl.BlockSpec(memory_space=pltpu.SMEM), vmem, vmem, vmem],
        out_specs=pl.BlockSpec(memory_space=pl.ANY),
        out_shape=jax.ShapeDtypeStruct((OWNED, WIDTH), jnp.bfloat16),
        scratch_shapes=[
            pltpu.VMEM((4, PART, WIDTH), jnp.float32),
            pltpu.VMEM((4, PART, WIDTH), jnp.bfloat16),
            pltpu.VMEM((OWNED, WIDTH), jnp.bfloat16),
            pltpu.SemaphoreType.DMA((PANELS,)),
        ],
        compiler_params=params(14),
        cost_estimate=light(),
        name="finish",
    )(place, sums, rest, last)


def wire_rows(rows):
    return rows * (WIDTH // LANES) + EXTRA


def put_coded(ref, value):
    largest = value
    while largest.shape != (1,) * value.ndim:
        axis = next(n for n, size in enumerate(largest.shape) if size > 1)
        largest = jnp.max(jnp.abs(largest), axis=axis, keepdims=True)
    power = jnp.ceil(jnp.log2(jnp.maximum(largest, 1e-30)))
    scaled = value * jnp.exp2(7 - power)
    scaled = scaled * jnp.abs(scaled)
    rows = value.shape[-2]
    for n in range(WIDTH // LANES):
        ref[..., n * rows : (n + 1) * rows, :] = scaled[..., n * LANES : (n + 1) * LANES]
    ref[..., ref.shape[-2] - EXTRA :, :] = jnp.broadcast_to(power, (*value.shape[:-2], EXTRA, LANES))


def decoded(ref):
    rows = (ref.shape[0] - EXTRA) * LANES // WIDTH
    value = jnp.concatenate([ref[n * rows : (n + 1) * rows, :] for n in range(WIDTH // LANES)], axis=1)
    power = ref[ref.shape[0] - EXTRA : ref.shape[0] - EXTRA + 1, 0:1]
    root = jnp.sqrt(jnp.abs(value)) * jnp.exp2(power - 7)
    return jnp.where(value < 0, -root, root)


def wire(value):
    return value.astype(WIRE)


def unwire(value):
    return value.astype(jnp.float32)


def small_kernel(kernel, shapes, mib, name):
    vmem = pl.BlockSpec(memory_space=pltpu.VMEM)
    shapes = [jax.ShapeDtypeStruct(shape, jnp.float32) for shape in shapes]
    return pl.pallas_call(
        kernel,
        out_specs=[vmem] * len(shapes),
        out_shape=shapes,
        compiler_params=params(mib),
        cost_estimate=light(),
        name=name,
    )


def add_cores_kernel(part, sibling, pair, out):
    for n in (0, 1, 2, 3):
        pair[n] = part[n] + sibling[3 - n]
    put_coded(out, pair[0])


def add_cores(part):
    call = small_kernel(add_cores_kernel, [part.shape, (wire_rows(part.shape[1]), LANES)], 12, "add_cores")
    return call(part, across_core(part))


def add_chips_kernel(pair, over, mine, out):
    mine[...] = pair[1] + decoded(over)
    put_coded(out, mine[...])


def add_chips(pair, over):
    call = small_kernel(add_chips_kernel, [pair.shape[1:], over.shape], 8, "add_chips")
    return call(pair, unwire(over))


def together(*values):
    return lax.optimization_barrier(values)


def on_device(amplitudes, integrals, tile_irrep, product_pairs, summed_pairs):
    row, col = lax.axis_index("row"), lax.axis_index("col")
    z = row // NX
    place = jnp.stack([row, col]).astype(jnp.int32)
    tables = (place, tile_irrep, product_pairs, summed_pairs)
    inner = (z == 1) | (z == 2)
    outward = {0: 1, 1: 0, 2: 3, 3: 2}
    inward = {1: 2, 2: 1}

    here0 = amplitudes
    beside0 = across_x(here0)
    here1 = along_z(here0, outward)
    middle = along_z(here0, inward)
    part0 = partial_ladder(tables, integrals, here0)
    beside0, here1, middle, part0 = together(beside0, here1, middle, part0)

    beside1 = across_x(here1)
    crossed = along_z(here1, inward)
    here2 = along_z(middle, outward)
    pair0, sent = add_cores(part0)
    over0 = across_y(wire(sent))
    part1 = partial_ladder(tables, integrals, beside0, here1)
    here2 = jnp.where(inner, middle, here2)
    beside1, crossed, here2, pair0, over0, part1 = together(beside1, crossed, here2, pair0, over0, part1)

    beside2 = across_x(here2)
    here3 = along_z(crossed, outward)
    mine0, sent = add_chips(pair0, over0)
    other0 = to_partner(wire(sent))
    pair1, sent = add_cores(part1)
    over1 = across_y(wire(sent))
    part2 = partial_ladder(tables, integrals, beside1, here2)
    own = sort_own(place, CHUNKS[0], pair0, mine0)
    owed_here = sort_owed(place, 0, pair0)
    here3 = jnp.where(inner, crossed, here3)
    beside2, here3, other0, own, owed_here, pair1, over1, part2 = together(
        beside2, here3, other0, own, owed_here, pair1, over1, part2
    )

    beside3 = across_x(here3)
    mine1, sent = add_chips(pair1, over1)
    other1 = to_partner(wire(sent))
    pair2, sent = add_cores(part2)
    over2 = across_y(wire(sent))
    part3 = partial_ladder(tables, integrals, beside2, here3)
    own = sort_own(place, CHUNKS[1], pair1, mine1, own)
    owed_beside = sort_owed(place, 0, pair1, across=1)
    owed_here = sort_owed(place, 1, pair1, owed_here)
    beside3, other0, other1, own, owed_here, owed_beside, pair2, over2, part3 = together(
        beside3, other0, other1, own, owed_here, owed_beside, pair2, over2, part3
    )

    mine2, sent = add_chips(pair2, over2)
    other2 = to_partner(wire(sent))
    pair3, sent = add_cores(part3)
    over3 = across_y(wire(sent))
    part4 = partial_ladder(tables, integrals, beside3)
    own = sort_own(place, CHUNKS[2], pair2, mine2, own)
    owed_beside = sort_owed(place, 1, pair2, owed_beside, across=1)
    owed_here = sort_owed(place, 2, pair2, owed_here)
    owed_beside = sort_owed(place, 2, pair3, owed_beside, across=1)
    owed_here = wire(sort_owed(place, 3, pair3, owed_here))
    other0, other1, other2, own, owed_here, owed_beside, pair3, over3, part4 = together(
        other0, other1, other2, own, owed_here, owed_beside, pair3, over3, part4
    )

    mine3, sent = add_chips(pair3, over3)
    sent, owed_here = together(wire(sent), owed_here)
    other3 = to_partner(sent)
    came_here = across_y(owed_here)
    pair4, sent = add_cores(part4)
    over4 = across_y(wire(sent))
    own = sort_own(place, CHUNKS[3], pair3, mine3, own)
    owed_beside = wire(sort_owed(place, 3, pair4, owed_beside, across=1))
    mine4, ready4 = add_chips(pair4, over4)
    other0, other1, other2, other3, own, pair4, mine4, ready4 = together(
        other0, other1, other2, other3, own, pair4, mine4, ready4
    )

    sent, *others = together(ready4, other0, other1, other2, other3)
    other4 = to_partner(wire(sent))
    came_beside = across_y(owed_beside)
    own = sort_own(place, CHUNKS[4], pair4, mine4, own)
    done = [turned(unwire(other)) for other in others]
    sums = gather(place, own, unwire(came_here), done)
    return finish(place, sums, unwire(came_beside), unwire(other4))


def solution(mesh):
    body = on_device if (mesh.shape["row"], mesh.shape["col"]) == (NZ * NX, NY * NC) else plain
    return jax.shard_map(
        body,
        mesh=mesh,
        in_specs=(P("row", "col"), P("col", "row"), P(), P("row", None), P("col", None)),
        out_specs=P("col", "row"),
        check_vma=False,
    )
```
